32 devices in a mesh: gx: 4 (over x, core), gy: 2 (over y), gz: 4 (over z).
Axes of the slice: x: 2, y: 2, z: 4, core: 2. Of those that a mesh axis runs over, the one named last changes fastest.
Arguments:
- bead_pos: float32 [3, 8, 8, 8, 128], P(None, 'gx', 'gy', 'gz'), may hold values from 0 to 3
- bead_vel: float32 [3, 8, 8, 8, 128], P(None, 'gx', 'gy', 'gz'), may hold values from -6 to 6
- bead_force: float32 [3, 8, 8, 8, 128], P(None, 'gx', 'gy', 'gz'), may hold values from -60 to 60
- cell_count: int32 [8, 8, 8], P('gx', 'gy', 'gz'), may hold values from 0 to 128
- pair_seed: int32 [8, 8, 8, 128], P('gx', 'gy', 'gz'), may hold values from 0 to 4095
- bead_half: int32 [8, 8, 8, 128], P('gx', 'gy', 'gz'), may hold values from 0 to 1
- grid_vel: float32 [3, 8, 8, 16], P(None, 'gx', ('gy', 'gz')), may hold values from -6 to 6
- correlation_map: int32 [8, 8, 16], P('gx', ('gy', 'gz')), may hold values 0 or 1
Outputs:
- new_positions: float32 [3, 8, 8, 8, 128], P(None, 'gx', 'gy', 'gz')
- new_velocities: float32 [3, 8, 8, 8, 128], P(None, 'gx', 'gy', 'gz')
- grid_velocity: float32 [3, 8, 8, 16], P(None, 'gx', ('gy', 'gz'))
- pressure: float32 [8, 8, 16], P('gx', ('gy', 'gz'))
- brick_velocity: float32 [3, 8, 8, 16], P(None, 'gx', 'gy', 'gz')
The draws below stay inside these ranges and needn't reach their ends.
Inputs may be any that keep to these rules, and one draw needn't show every extreme that they name: `cell_count`: slots below a cell's count hold beads, the others are padding.
All inputs are finite; a program needn't handle non-finite values. No bound on the sum of `correlation_map` on one device may be relied on, other than what follows from the above.
Results may differ from the reference program's by a relative error of at most 0.0003.
Values sent between devices are 32-bit elements; how exact they have to be, the bound alone decides.
A program may use at most 64 MiB of HBM per device.

```python
import math
import jax
import jax.numpy as jnp
import numpy as np
from jax import lax

SLOTS = 128
STEPS = 2
ITERS = 4
NCX = 8
NCY = 8
NCZ = 8
BINS_Z = 16


def set_ends(values, own_key, least, high):
    index_at = [jax.random.randint(jax.random.fold_in(own_key, axis), (), 0, length) for axis, length in enumerate(values.shape)]
    main_axis = values.shape.index(max(values.shape))
    next_to = index_at[:main_axis] + [(index_at[main_axis] + 1) % values.shape[main_axis]] + index_at[main_axis + 1:]
    return values.at[tuple(index_at)].set(least).at[tuple(next_to)].set(high)


def block_levels(stream_key, dims, cuts, low, high):
    def one(dim, blocks):
        heights = jax.random.uniform(jax.random.fold_in(jax.random.fold_in(stream_key, 6), dim), (blocks,), jnp.float32, low / len(cuts), high / len(cuts))
        return jnp.repeat(jnp.exp(heights), dims[dim] // blocks).reshape((-1,) + (1,) * (len(dims) - dim - 1))

    gain = one(*cuts[0])
    for cut in cuts[1:]:
        gain = gain * one(*cut)
    return gain


def gaussian(key, shape, scale, bound, cuts=(), held_as=jnp.bfloat16):
    entries = jax.random.normal(key, shape, jnp.float32) * scale
    if len(cuts) > 0:
        entries = block_levels(key, shape, cuts, -0.22, 0.18) * entries
    return jnp.clip(entries, min=-bound, max=bound).astype(held_as)


def setup_inputs(seed: int = 0) -> dict:
    key_list = jax.random.split(jax.random.key(seed), 9)
    return {
        "bead_pos": jnp.clip(3.0 * jax.random.uniform(key_list[0], (3, NCX, NCY, NCZ, SLOTS), jnp.float32) ** block_levels(key_list[0], (3, NCX, NCY, NCZ, SLOTS), ((1, 4), (2, 2), (3, 4)), -0.2, 0.2), 0.0, 3.0),
        "bead_vel": gaussian(key_list[1], (3, NCX, NCY, NCZ, SLOTS), 1.0, 6.0, ((1, 4), (2, 2), (3, 4)), jnp.float32),
        "bead_force": gaussian(key_list[2], (3, NCX, NCY, NCZ, SLOTS), 10.0, 60.0, ((1, 4), (2, 2), (3, 4)), jnp.float32),
        "cell_count": set_ends(jax.random.randint(key_list[3], (NCX, NCY, NCZ), 0, SLOTS + 1), jax.random.fold_in(key_list[3], 1), 0, SLOTS).astype(jnp.int32),
        "pair_seed": set_ends(jax.random.randint(key_list[4], (NCX, NCY, NCZ, SLOTS), 0, 4096), jax.random.fold_in(key_list[4], 1), 0, 4095).astype(jnp.int32),
        "bead_half": set_ends(jax.random.randint(key_list[5], (NCX, NCY, NCZ, SLOTS), 0, 2), jax.random.fold_in(key_list[5], 1), 0, 1).astype(jnp.int32),
        "grid_vel": gaussian(key_list[6], (3, NCX, NCY, BINS_Z), 1.0, 6.0, ((1, 4), (2, 8)), jnp.float32),
        "correlation_map": set_ends((jax.random.randint(key_list[7], (NCX, NCY, BINS_Z), 0, 2) < 1).astype(jnp.int32), jax.random.fold_in(key_list[7], 1), 0, 1),
    }


cell_edge = 3.0
conserve = 25.0
friction = 4.5
noise_scale = 3.0 * math.sqrt(12.0) / math.sqrt(0.04)
time_step = 0.04
predict_weight = 0.65
couple_rate = 0.5
hash_prime = 4093

def pair_sum(center, padded, step_tag):
    extent_x, extent_y, extent_z = (center.shape[1], center.shape[2], center.shape[3])
    slot_count = center.shape[4]
    seed_own = center[6].astype(jnp.int32)[..., :, None]
    offsets_y = np.repeat(np.array([oy for oy in (-1, 0, 1) for oz in (-1, 0, 1)]), slot_count)
    offsets_z = np.repeat(np.array([oz for oy in (-1, 0, 1) for oz in (-1, 0, 1)]), slot_count)
    shift_y = jnp.asarray(offsets_y * cell_edge, dtype=jnp.float32)
    shift_z = jnp.asarray(offsets_z * cell_edge, dtype=jnp.float32)
    totals = [jnp.zeros(center.shape[1:], jnp.float32) for axis_k in range(3)]
    for offset_x in (-1, 0, 1):
        pieces = []
        for offset_y in (-1, 0, 1):
            for offset_z in (-1, 0, 1):
                pieces.append(padded[:, 1 + offset_x:1 + offset_x + extent_x, 1 + offset_y:1 + offset_y + extent_y, 1 + offset_z:1 + offset_z + extent_z, :])
        nearby = jnp.concatenate(pieces, axis=-1)
        shifts = (cell_edge * offset_x, shift_y, shift_z)
        deltas = [center[axis_k][..., :, None] - nearby[axis_k][..., None, :] - shifts[axis_k] for axis_k in range(3)]
        square = deltas[0] * deltas[0] + deltas[1] * deltas[1] + deltas[2] * deltas[2]
        weight = jnp.maximum(1.0 - square, 0.0) * nearby[7][..., None, :]
        closing = deltas[0] * (center[3][..., :, None] - nearby[3][..., None, :])
        closing = closing + deltas[1] * (center[4][..., :, None] - nearby[4][..., None, :])
        closing = closing + deltas[2] * (center[5][..., :, None] - nearby[5][..., None, :])
        seed_other = nearby[6].astype(jnp.int32)[..., None, :]
        hashed = jnp.remainder(seed_own * seed_other + (seed_own + seed_other) * step_tag, hash_prime)
        random_term = (hashed.astype(jnp.float32) / hash_prime - 0.5) * noise_scale
        strength = weight * (conserve + random_term) - friction * weight * weight * closing
        for axis_k in range(3):
            totals[axis_k] = totals[axis_k] + lax.optimization_barrier(jnp.sum(strength * deltas[axis_k], axis=-1))
    return jnp.stack(totals) * center[7]

def pad_domain(field):
    wrapped = jnp.pad(field, [(0, 0), (1, 1)] + [(0, 0)] * (field.ndim - 2), mode='wrap')
    return jnp.pad(wrapped, [(0, 0), (0, 0), (1, 1), (1, 1)] + [(0, 0)] * (field.ndim - 4))

def all_forces(stacked, step_tag):
    padded = pad_domain(stacked)

    def plane(index):
        block_rows = lax.dynamic_slice_in_dim(padded, index, 3, 1)
        return pair_sum(block_rows[:, 1:2, 1:-1, 1:-1], block_rows, step_tag)[:, 0]
    planes = lax.map(plane, jnp.arange(NCX, dtype=jnp.int32))
    return jnp.moveaxis(planes, 0, 1)

def bin_sums(velocity, occupied, bead_half):
    pieces = []
    for side_index in (0, 1):
        select = occupied * (bead_half == side_index).astype(jnp.float32)
        moments = lax.optimization_barrier(jnp.sum(velocity * select[None], axis=-1))
        counted = lax.optimization_barrier(jnp.sum(select, axis=-1))
        pieces.append(jnp.concatenate([moments, counted[None]], axis=0))
    joined = jnp.stack(pieces, axis=-1)
    extent = joined.shape
    return joined.reshape(extent[0], extent[1], extent[2], extent[3] * 2)

def couple(bin_totals, grid_field, coupled_flag):
    bin_mean = bin_totals[:3] / jnp.maximum(bin_totals[3], 1.0)
    return grid_field + couple_rate * coupled_flag * (bin_mean - grid_field)

def project(coupled_vel, pad, reduce_all):
    padded = pad(coupled_vel)
    divergence = padded[0, 2:, 1:-1, 1:-1] - padded[0, :-2, 1:-1, 1:-1]
    divergence = divergence + padded[1, 1:-1, 2:, 1:-1] - padded[1, 1:-1, :-2, 1:-1]
    divergence = 0.5 * (divergence + padded[2, 1:-1, 1:-1, 2:] - padded[2, 1:-1, 1:-1, :-2])

    def operate(field):
        beside_all = pad(field[None])[0]
        beside = beside_all[2:, 1:-1, 1:-1] + beside_all[:-2, 1:-1, 1:-1]
        beside = beside + beside_all[1:-1, 2:, 1:-1] + beside_all[1:-1, :-2, 1:-1]
        beside = beside + beside_all[1:-1, 1:-1, 2:] + beside_all[1:-1, 1:-1, :-2]
        return 6.0 * field - beside
    residual = -divergence
    direction = residual
    pressure = jnp.zeros_like(residual)
    norm_now = reduce_all(residual * residual)
    for repeat in range(ITERS):
        applied = operate(direction)
        step_length = norm_now / reduce_all(direction * applied)
        pressure = pressure + step_length * direction
        residual = residual - step_length * applied
        norm_next = reduce_all(residual * residual)
        direction = residual + norm_next / norm_now * direction
        norm_now = norm_next
    beside_all = pad(pressure[None])[0]
    gradient = jnp.stack([beside_all[2:, 1:-1, 1:-1] - beside_all[:-2, 1:-1, 1:-1], beside_all[1:-1, 2:, 1:-1] - beside_all[1:-1, :-2, 1:-1], beside_all[1:-1, 1:-1, 2:] - beside_all[1:-1, 1:-1, :-2]])
    return (coupled_vel - 0.5 * gradient, pressure)

def reference(bead_pos, bead_vel, bead_force, cell_count, pair_seed, bead_half, grid_vel, correlation_map):
    occupied = (lax.broadcasted_iota(jnp.int32, pair_seed.shape, 3) < cell_count[..., None]).astype(jnp.float32)
    static = jnp.stack([pair_seed.astype(jnp.float32), occupied])
    position, velocity, current = (bead_pos, bead_vel, bead_force)
    for step_number in range(STEPS):
        step_tag = step_number + 3
        position = position + time_step * velocity + 0.5 * time_step * time_step * current
        guessed = velocity + predict_weight * time_step * current
        predicted = all_forces(jnp.concatenate([position, guessed, static]), step_tag)
        corrected = velocity + 0.5 * time_step * (current + predicted)
        iterated = all_forces(jnp.concatenate([position, corrected, static]), step_tag)
        velocity = velocity + 0.5 * time_step * (current + iterated)
        current = iterated
    bin_totals = bin_sums(velocity, occupied, bead_half)
    coupled_vel = couple(bin_totals, grid_vel, correlation_map.astype(jnp.float32))
    grid_velocity, pressure = project(coupled_vel, pad_domain, jnp.sum)
    return (position, velocity, grid_velocity, pressure, grid_velocity)
```

```python
import functools
import math

import jax
import jax.numpy as jnp
import numpy as np
from jax import lax
from jax.experimental import pallas as pl
from jax.experimental.pallas import tpu as pltpu
from jax.sharding import PartitionSpec as P

STEPS = 2
ITERS = 4

cell_edge = 3.0
conserve = 25.0
friction = 4.5
noise_scale = 3.0 * math.sqrt(12.0) / math.sqrt(0.04)
time_step = 0.04
predict_weight = 0.65
couple_rate = 0.5
hash_prime = 4093

LANES = 128
ROWS = 8
BLOCK = 32
FAR = 1.0e15
NEAR = [(ox, oy, oz) for ox in (-1, 0, 1) for oy in (-1, 0, 1) for oz in (-1, 0, 1)]


def pair_terms(own, chunk, step_tag):
    deltas = [own[k] - chunk[k] for k in range(3)]
    square = deltas[0] * deltas[0] + deltas[1] * deltas[1] + deltas[2] * deltas[2]
    weight = jnp.maximum(1.0 - square, 0.0)
    closing = deltas[0] * (own[3] - chunk[3])
    closing = closing + deltas[1] * (own[4] - chunk[4])
    closing = closing + deltas[2] * (own[5] - chunk[5])
    turns = own[6] * chunk[6] + (0.5 - step_tag * step_tag) / hash_prime
    part = turns - jnp.floor(turns)
    steady = part * noise_scale + (conserve - (0.5 + 0.5 / hash_prime) * noise_scale)
    strength = weight * (steady - weight * closing)
    return [strength * deltas[k] for k in range(3)]


def centred(seed, step_tag):
    moved = seed + float(step_tag)
    return jnp.where(moved > 2046.0, moved - float(hash_prime), moved)


def force_kernel(
    step_tag, closing_eval, count_ref, padded_ref, state_ref, tile_out, state_out,
    rows_x, masks, index_rows, base_vec, base_smem, list_ref, own_cols, force_cols, copy_sem,
):
    px, py, pz = padded_ref.shape[:3]
    cx, cy, cz = px - 2, py - 2, pz - 2
    cells = cx * cy * cz
    lane = lax.broadcasted_iota(jnp.int32, (ROWS, LANES), 1)

    for ix in range(px):
        for iz in range(pz):
            present = padded_ref[ix, :, iz, 7, :] > 0.5
            for k in range(3):
                rows_x[k, ix, iz, 0:py, :] = jnp.where(present, padded_ref[ix, :, iz, k, :], FAR)

    for ix in range(cx):
        for iz in range(cz):
            row = (ix * cz + iz) * cy
            low, high = [], []
            for k in range(3):
                mine = rows_x[k, 1 + ix, 1 + iz, 1 : 1 + cy, :]
                there = mine < 0.1 * FAR
                least = jnp.min(jnp.where(there, mine, FAR), axis=1, keepdims=True)
                most = jnp.max(jnp.where(there, mine, -FAR), axis=1, keepdims=True)
                low.append(least - 1.001 - 1e-6 * jnp.abs(least))
                high.append(most + 1.001 + 1e-6 * jnp.abs(most))
            for n, offset in enumerate(NEAR):
                keep = None
                for k in range(3):
                    near = rows_x[
                        k, 1 + ix + offset[0], 1 + iz + offset[2], 1 + offset[1] : 1 + offset[1] + cy, :
                    ] + cell_edge * offset[k]
                    inside = (near >= low[k]) & (near <= high[k])
                    keep = inside if keep is None else keep & inside
                masks[n * cells + row : n * cells + row + cy, :] = jnp.where(keep, 1.0, 0.0)

    mask = masks[...]
    before = lax.broadcasted_iota(jnp.int32, (LANES, LANES), 0)
    after = lax.broadcasted_iota(jnp.int32, (LANES, LANES), 1)
    upper = jnp.where(before < after, 1.0, 0.0).astype(jnp.bfloat16)
    ones = jnp.ones((LANES, LANES), jnp.bfloat16)
    mask16 = mask.astype(jnp.bfloat16)
    rank = jnp.dot(mask16, upper, preferred_element_type=jnp.float32).astype(jnp.int32)
    count = jnp.dot(mask16, ones, preferred_element_type=jnp.float32).astype(jnp.int32)
    spot = lax.broadcasted_iota(jnp.int32, mask.shape, 1)
    entry = jnp.where(mask > 0.5, (spot - rank) * LANES + spot, spot)
    for bit in range(7):
        width = 1 << bit
        flag = LANES << bit
        moved = pltpu.roll(entry, LANES - width, 1)
        stay = jnp.where((entry & flag) != 0, entry & (LANES - 1), entry)
        entry = jnp.where((moved & flag) != 0, moved, stay)
    entry = entry & (LANES - 1)
    bases = []
    running = jnp.zeros((cells, LANES), jnp.int32)
    table = jnp.zeros((cells, LANES), jnp.int32)
    spot_cells = lax.broadcasted_iota(jnp.int32, (cells, LANES), 1)
    for n in range(len(NEAR)):
        bases.append(running)
        table = jnp.where(spot_cells == n, running, table)
        running = running + count[n * cells : (n + 1) * cells, :]
    table = jnp.where(spot_cells == len(NEAR), running, table)
    base_vec[...] = table
    to_smem = pltpu.make_async_copy(base_vec, base_smem, copy_sem)
    to_smem.start()
    base_all = jnp.concatenate(bases, axis=0)
    for bit in range(7):
        width = 1 << bit
        entry = jnp.where((base_all & width) != 0, pltpu.roll(entry, width, 1), entry)
    index_rows[...] = entry
    to_smem.wait()

    row_id = lax.broadcasted_iota(jnp.int32, (ROWS, LANES), 0)
    lane_block = lax.broadcasted_iota(jnp.int32, (BLOCK, LANES), 1)
    zero = jnp.zeros((BLOCK, LANES), jnp.float32)

    def one_cell(cell, carry):
        ix = cell // (cy * cz)
        iz = (cell // cy) % cz
        iy = cell % cy
        current = jnp.zeros((ROWS, LANES), jnp.float32)
        for n, offset in enumerate(NEAR):
            tile = padded_ref[ix + 1 + offset[0], iy + 1 + offset[1], iz + 1 + offset[2]]
            index = jnp.broadcast_to(index_rows[pl.ds(n * cells + cell, 1), :], (ROWS, LANES))
            found = jnp.take_along_axis(tile, index, axis=1)
            for k in range(3):
                if offset[k] != 0:
                    found = jnp.where(row_id == k, found + cell_edge * offset[k], found)
            base = base_smem[cell, n]
            following = base_smem[cell, n + 1]
            merged = jnp.where(lane >= (base & (LANES - 1)), found, current)
            list_ref[base >> 7] = merged
            crossed = (following >> 7) > (base >> 7)
            current = jnp.where(crossed, found, merged)
        total = base_smem[cell, len(NEAR)]
        list_ref[total >> 7] = current
        chunks = (total + LANES - 1) >> 7
        own_tile = padded_ref[ix + 1, iy + 1, iz + 1]
        own_cols[...] = own_tile.T
        blocks = (count_ref[ix, iy, iz] + BLOCK - 1) // BLOCK

        def one_block(block, carry):
            at = pl.multiple_of(block * BLOCK, BLOCK)
            cols = own_cols[pl.ds(at, BLOCK), :]
            own = [jnp.broadcast_to(cols[:, k : k + 1], (BLOCK, LANES)) for k in range(7)]
            for k in range(3, 6):
                own[k] = own[k] * friction
            own[6] = centred(own[6], step_tag)

            def one_chunk(index, sums):
                tile = list_ref[index]
                chunk = [tile[k : k + 1, :] for k in range(7)]
                valid = lane[0:1, :] + index * LANES < total
                chunk[0] = jnp.where(valid, chunk[0], -FAR)
                for k in range(3, 6):
                    chunk[k] = chunk[k] * friction
                chunk[6] = centred(chunk[6], step_tag) * (1.0 / hash_prime)
                terms = pair_terms(own, chunk, step_tag)
                return tuple(sums[k] + terms[k] for k in range(3))

            sums = lax.fori_loop(0, chunks, one_chunk, (zero, zero, zero))
            folded = [jnp.sum(part, axis=1, keepdims=True) for part in sums]
            force_cols[pl.ds(at, BLOCK), :] = jnp.where(
                lane_block == 0, folded[0], jnp.where(lane_block == 1, folded[1], folded[2])
            )
            return carry

        lax.fori_loop(0, blocks, one_block, 0)
        force = force_cols[...].T[0:3, :]
        force = jnp.where(own_tile[7:8, :] > 0.5, force, 0.0)
        state = state_ref[ix, iy, iz]
        vel, old = state[0:3, :], state[3:6, :]
        new_vel = vel + 0.5 * time_step * (old + force)
        if closing_eval:
            position = own_tile[0:3, :]
            position = position + time_step * new_vel + 0.5 * time_step * time_step * force
            guessed = new_vel + predict_weight * time_step * force
            state_out[ix, iy, iz, 0:3, :] = new_vel
            state_out[ix, iy, iz, 3:6, :] = force
            state_out[ix, iy, iz, 6:8, :] = own_tile[6:8, :]
            tile_out[ix, iy, iz, 0:3, :] = position
            tile_out[ix, iy, iz, 3:6, :] = guessed
        else:
            state_out[ix, iy, iz] = state
            tile_out[ix, iy, iz, 0:3, :] = own_tile[0:3, :]
            tile_out[ix, iy, iz, 3:6, :] = new_vel
        tile_out[ix, iy, iz, 6:8, :] = own_tile[6:8, :]
        return carry

    lax.fori_loop(0, cells, one_cell, 0)


def force_call(step_tag, closing_eval, cell_count, padded, state):
    px, py, pz = padded.shape[:3]
    cx, cy, cz = state.shape[:3]
    cells = cx * cy * cz
    near = len(NEAR)
    tall = -(-py // 8) * 8
    return pl.pallas_call(
        functools.partial(force_kernel, step_tag, closing_eval),
        out_shape=(
            jax.ShapeDtypeStruct(state.shape, jnp.float32),
            jax.ShapeDtypeStruct(state.shape, jnp.float32),
        ),
        in_specs=[
            pl.BlockSpec(memory_space=pltpu.SMEM),
            pl.BlockSpec(memory_space=pltpu.VMEM),
            pl.BlockSpec(memory_space=pltpu.VMEM),
        ],
        out_specs=(
            pl.BlockSpec(memory_space=pltpu.VMEM),
            pl.BlockSpec(memory_space=pltpu.VMEM),
        ),
        scratch_shapes=[
            pltpu.VMEM((3, px, pz, tall, LANES), jnp.float32),
            pltpu.VMEM((near * cells, LANES), jnp.float32),
            pltpu.VMEM((near * cells, LANES), jnp.int32),
            pltpu.VMEM((cells, LANES), jnp.int32),
            pltpu.SMEM((cells, LANES), jnp.int32),
            pltpu.VMEM((near + 1, ROWS, LANES), jnp.float32),
            pltpu.VMEM((LANES, ROWS), jnp.float32),
            pltpu.VMEM((LANES, LANES), jnp.float32),
            pltpu.SemaphoreType.DMA,
        ],
        compiler_params=pltpu.CompilerParams(vmem_limit_bytes=32 * 1024 * 1024),
    )(cell_count, padded, state)


def with_halo(block, sides, width, periodic):
    for axis, dim in sides:
        count = lax.axis_size(axis)
        forward = [(i, i + 1) for i in range(count - 1)]
        if periodic:
            forward.append((count - 1, 0))
        backward = [(target, source) for source, target in forward]
        low = lax.ppermute(
            lax.slice_in_dim(block, block.shape[dim] - width, None, axis=dim), axis, forward
        )
        high = lax.ppermute(lax.slice_in_dim(block, 0, width, axis=dim), axis, backward)
        block = jnp.concatenate([low, block, high], axis=dim)
    return block


def pad_domain(field):
    wrapped = jnp.pad(field, [(0, 0), (1, 1)] + [(0, 0)] * (field.ndim - 2), mode="wrap")
    return jnp.pad(wrapped, [(0, 0), (0, 0), (1, 1), (1, 1)] + [(0, 0)] * (field.ndim - 4))


def bin_sums(velocity, occupied, bead_half):
    pieces = []
    for side_index in (0, 1):
        select = occupied * (bead_half == side_index).astype(jnp.float32)
        moments = jnp.sum(velocity * select[None], axis=-1)
        counted = jnp.sum(select, axis=-1)
        pieces.append(jnp.concatenate([moments, counted[None]], axis=0))
    joined = jnp.stack(pieces, axis=-1)
    extent = joined.shape
    return joined.reshape(extent[0], extent[1], extent[2], extent[3] * 2)


def couple(bin_totals, grid_field, coupled_flag):
    bin_mean = bin_totals[:3] / jnp.maximum(bin_totals[3], 1.0)
    return grid_field + couple_rate * coupled_flag * (bin_mean - grid_field)


def project(coupled_vel, pad, reduce_all):
    padded = pad(coupled_vel)
    divergence = padded[0, 2:, 1:-1, 1:-1] - padded[0, :-2, 1:-1, 1:-1]
    divergence = divergence + padded[1, 1:-1, 2:, 1:-1] - padded[1, 1:-1, :-2, 1:-1]
    divergence = 0.5 * (divergence + padded[2, 1:-1, 1:-1, 2:] - padded[2, 1:-1, 1:-1, :-2])
    residual = -divergence
    direction = residual
    pressure = jnp.zeros_like(residual)
    norm_now = reduce_all(residual * residual)
    for repeat in range(ITERS):
        operate_beside_all = pad(direction[None])[0]
        beside = operate_beside_all[2:, 1:-1, 1:-1] + operate_beside_all[:-2, 1:-1, 1:-1]
        beside = beside + operate_beside_all[1:-1, 2:, 1:-1] + operate_beside_all[1:-1, :-2, 1:-1]
        beside = beside + operate_beside_all[1:-1, 1:-1, 2:] + operate_beside_all[1:-1, 1:-1, :-2]
        applied = 6.0 * direction - beside
        step_length = norm_now / reduce_all(direction * applied)
        pressure = pressure + step_length * direction
        residual = residual - step_length * applied
        norm_next = reduce_all(residual * residual)
        direction = residual + norm_next / norm_now * direction
        norm_now = norm_next
    beside_all = pad(pressure[None])[0]
    gradient = jnp.stack(
        [
            beside_all[2:, 1:-1, 1:-1] - beside_all[:-2, 1:-1, 1:-1],
            beside_all[1:-1, 2:, 1:-1] - beside_all[1:-1, :-2, 1:-1],
            beside_all[1:-1, 1:-1, 2:] - beside_all[1:-1, 1:-1, :-2],
        ]
    )
    return (coupled_vel - 0.5 * gradient, pressure)


def per_device(
    bead_pos, bead_vel, bead_force, cell_count, pair_seed, bead_half, grid_vel, correlation_map
):
    occupied = (lax.broadcasted_iota(jnp.int32, pair_seed.shape, 3) < cell_count[..., None]).astype(
        jnp.float32
    )
    def tiled(parts):
        return jnp.moveaxis(jnp.concatenate(parts), 0, 3)

    def gather_beads(tile):
        along_x = with_halo(tile, (("gx", 0),), 1, True)
        return with_halo(along_x, (("gy", 1), ("gz", 2)), 1, False)

    static = jnp.stack([pair_seed.astype(jnp.float32), occupied])
    tile = tiled(
        [
            bead_pos + time_step * bead_vel + 0.5 * time_step * time_step * bead_force,
            bead_vel + predict_weight * time_step * bead_force,
            static,
        ]
    )
    state = tiled([bead_vel, bead_force, static])
    for step_number in range(STEPS):
        step_tag = step_number + 3
        tile, state = force_call(step_tag, False, cell_count, gather_beads(tile), state)
        position = jnp.moveaxis(tile[..., 0:3, :], 3, 0)
        tile, state = force_call(step_tag, True, cell_count, gather_beads(tile), state)
    velocity = jnp.moveaxis(state[..., 0:3, :], 3, 0)
    bin_totals = bin_sums(velocity, occupied, bead_half)
    coupled_flag = correlation_map.astype(jnp.float32)
    along_z = lax.all_gather(bin_totals, "gz", axis=3, tiled=True)
    along_y = lax.all_gather(along_z, "gy", axis=2, tiled=True)
    grid_rows = lax.all_gather(
        jnp.concatenate([grid_vel, coupled_flag[None]]), ("gy", "gz"), axis=2, tiled=True
    )
    whole_bins, whole_grid = (
        lax.all_gather(along_y, "gx", axis=1, tiled=True),
        lax.all_gather(grid_rows, "gx", axis=1, tiled=True),
    )
    coupled_vel = couple(whole_bins, whole_grid[:3], whole_grid[3])
    full_velocity, full_pressure = project(coupled_vel, pad_domain, jnp.sum)
    rows_x = lax.axis_index("gx") * grid_vel.shape[1]
    owner_rows = (
        lax.axis_index("gy") * lax.axis_size("gz") + lax.axis_index("gz")
    ) * grid_vel.shape[2]
    grid_velocity = lax.dynamic_slice(full_velocity, (0, rows_x, owner_rows, 0), grid_vel.shape)
    pressure = lax.dynamic_slice(full_pressure, (rows_x, owner_rows, 0), correlation_map.shape)
    brick_rows = lax.axis_index("gy") * bin_totals.shape[2]
    brick_depth = lax.axis_index("gz") * bin_totals.shape[3]
    brick_velocity = lax.dynamic_slice(
        full_velocity,
        (0, rows_x, brick_rows, brick_depth),
        (3, bin_totals.shape[1], bin_totals.shape[2], bin_totals.shape[3]),
    )
    return (position, velocity, grid_velocity, pressure, brick_velocity)


def solution(mesh):
    placed = (
        P(None, "gx", "gy", "gz", None),
        P(None, "gx", "gy", "gz", None),
        P(None, "gx", "gy", "gz", None),
        P("gx", "gy", "gz"),
        P("gx", "gy", "gz", None),
        P("gx", "gy", "gz", None),
        P(None, "gx", ("gy", "gz"), None),
        P("gx", ("gy", "gz"), None),
    )
    return jax.shard_map(
        per_device,
        mesh=mesh,
        in_specs=placed,
        out_specs=(
            P(None, "gx", "gy", "gz", None),
            P(None, "gx", "gy", "gz", None),
            P(None, "gx", ("gy", "gz"), None),
            P("gx", ("gy", "gz"), None),
            P(None, "gx", "gy", "gz"),
        ),
        check_vma=False,
    )
```

```python
import functools
import math

import jax
import jax.numpy as jnp
from jax import lax
from jax.experimental import pallas as pl
from jax.experimental.pallas import tpu as pltpu
from jax.sharding import PartitionSpec as P

STEPS = 2
ITERS = 4

cell_edge = 3.0
conserve = 25.0
friction = 4.5
noise_scale = 3.0 * math.sqrt(12.0) / math.sqrt(0.04)
time_step = 0.04
predict_weight = 0.65
couple_rate = 0.5
hash_prime = 4093

LANES = 128
ROWS = 8
BLOCK = 32
FAR = 1.0e15
NEAR = [(ox, oy, oz) for ox in (-1, 0, 1) for oy in (-1, 0, 1) for oz in (-1, 0, 1)]


def pair_terms(own, chunk, step_tag):
    deltas = [own[k] - chunk[k] for k in range(3)]
    square = deltas[0] * deltas[0] + deltas[1] * deltas[1] + deltas[2] * deltas[2]
    weight = jnp.maximum(1.0 - square, 0.0)
    closing = deltas[0] * (own[3] - chunk[3])
    closing = closing + deltas[1] * (own[4] - chunk[4])
    closing = closing + deltas[2] * (own[5] - chunk[5])
    turns = own[6] * chunk[6] + (0.5 - step_tag * step_tag) / hash_prime
    part = turns - jnp.floor(turns)
    steady = part * noise_scale + (conserve - (0.5 + 0.5 / hash_prime) * noise_scale)
    strength = weight * (steady - weight * closing)
    return [strength * deltas[k] for k in range(3)]


def centred(seed, step_tag):
    moved = seed + float(step_tag)
    return jnp.where(moved > 2046.0, moved - float(hash_prime), moved)


def force_kernel(
    step_tag, closing_eval, count_ref, padded_ref, state_ref, tile_out, state_out, *rest,
):
    (rows_x, masks, index_rows, base_vec, base_smem, list_ref, own_cols, force_cols, copy_sem) = (
        rest[-9:]
    )
    px, py, pz = padded_ref.shape[:3]
    cx, cy, cz = px - 2, py - 2, pz - 2
    cells = cx * cy * cz
    lane = lax.broadcasted_iota(jnp.int32, (ROWS, LANES), 1)

    for ix in range(px):
        for iz in range(pz):
            present = padded_ref[ix, :, iz, 7, :] > 0.5
            for k in range(3):
                rows_x[k, ix, iz, 0:py, :] = jnp.where(present, padded_ref[ix, :, iz, k, :], FAR)

    for ix in range(cx):
        for iz in range(cz):
            row = (ix * cz + iz) * cy
            low, high = [], []
            for k in range(3):
                mine = rows_x[k, 1 + ix, 1 + iz, 1 : 1 + cy, :]
                there = mine < 0.1 * FAR
                least = jnp.min(jnp.where(there, mine, FAR), axis=1, keepdims=True)
                most = jnp.max(jnp.where(there, mine, -FAR), axis=1, keepdims=True)
                low.append(least - 1.001 - 1e-6 * jnp.abs(least))
                high.append(most + 1.001 + 1e-6 * jnp.abs(most))
            for n, offset in enumerate(NEAR):
                keep = None
                for k in range(3):
                    near = rows_x[
                        k, 1 + ix + offset[0], 1 + iz + offset[2], 1 + offset[1] : 1 + offset[1] + cy, :
                    ] + cell_edge * offset[k]
                    inside = (near >= low[k]) & (near <= high[k])
                    keep = inside if keep is None else keep & inside
                masks[n * cells + row : n * cells + row + cy, :] = jnp.where(keep, 1.0, 0.0)

    mask = masks[...]
    before = lax.broadcasted_iota(jnp.int32, (LANES, LANES), 0)
    after = lax.broadcasted_iota(jnp.int32, (LANES, LANES), 1)
    upper = jnp.where(before < after, 1.0, 0.0).astype(jnp.bfloat16)
    ones = jnp.ones((LANES, LANES), jnp.bfloat16)
    mask16 = mask.astype(jnp.bfloat16)
    rank = jnp.dot(mask16, upper, preferred_element_type=jnp.float32).astype(jnp.int32)
    count = jnp.dot(mask16, ones, preferred_element_type=jnp.float32).astype(jnp.int32)
    spot = lax.broadcasted_iota(jnp.int32, mask.shape, 1)
    entry = jnp.where(mask > 0.5, (spot - rank) * LANES + spot, spot)
    for bit in range(7):
        width = 1 << bit
        flag = LANES << bit
        moved = pltpu.roll(entry, LANES - width, 1)
        stay = jnp.where((entry & flag) != 0, entry & (LANES - 1), entry)
        entry = jnp.where((moved & flag) != 0, moved, stay)
    entry = entry & (LANES - 1)
    bases = []
    running = jnp.zeros((cells, LANES), jnp.int32)
    table = jnp.zeros((cells, LANES), jnp.int32)
    spot_cells = lax.broadcasted_iota(jnp.int32, (cells, LANES), 1)
    for n in range(len(NEAR)):
        bases.append(running)
        table = jnp.where(spot_cells == n, running, table)
        running = running + count[n * cells : (n + 1) * cells, :]
    table = jnp.where(spot_cells == len(NEAR), running, table)
    base_vec[...] = table
    to_smem = pltpu.make_async_copy(base_vec, base_smem, copy_sem)
    to_smem.start()
    base_all = jnp.concatenate(bases, axis=0)
    for bit in range(7):
        width = 1 << bit
        entry = jnp.where((base_all & width) != 0, pltpu.roll(entry, width, 1), entry)
    index_rows[...] = entry
    to_smem.wait()

    row_id = lax.broadcasted_iota(jnp.int32, (ROWS, LANES), 0)
    lane_block = lax.broadcasted_iota(jnp.int32, (BLOCK, LANES), 1)
    zero = jnp.zeros((BLOCK, LANES), jnp.float32)

    def one_cell(cell, carry):
        ix = cell // (cy * cz)
        iz = (cell // cy) % cz
        iy = cell % cy
        current = jnp.zeros((ROWS, LANES), jnp.float32)
        for n, offset in enumerate(NEAR):
            tile = padded_ref[ix + 1 + offset[0], iy + 1 + offset[1], iz + 1 + offset[2]]
            index = jnp.broadcast_to(index_rows[pl.ds(n * cells + cell, 1), :], (ROWS, LANES))
            found = jnp.take_along_axis(tile, index, axis=1)
            for k in range(3):
                if offset[k] != 0:
                    found = jnp.where(row_id == k, found + cell_edge * offset[k], found)
            base = base_smem[cell, n]
            following = base_smem[cell, n + 1]
            merged = jnp.where(lane >= (base & (LANES - 1)), found, current)
            list_ref[base >> 7] = merged
            crossed = (following >> 7) > (base >> 7)
            current = jnp.where(crossed, found, merged)
        total = base_smem[cell, len(NEAR)]
        list_ref[total >> 7] = current
        chunks = (total + LANES - 1) >> 7
        own_tile = padded_ref[ix + 1, iy + 1, iz + 1]
        own_cols[...] = own_tile.T
        blocks = (count_ref[ix, iy, iz] + BLOCK - 1) // BLOCK

        def one_block(block, carry):
            at = pl.multiple_of(block * BLOCK, BLOCK)
            cols = own_cols[pl.ds(at, BLOCK), :]
            own = [jnp.broadcast_to(cols[:, k : k + 1], (BLOCK, LANES)) for k in range(7)]
            for k in range(3, 6):
                own[k] = own[k] * friction
            own[6] = centred(own[6], step_tag)

            def one_chunk(index, sums):
                tile = list_ref[index]
                chunk = [tile[k : k + 1, :] for k in range(7)]
                valid = lane[0:1, :] + index * LANES < total
                chunk[0] = jnp.where(valid, chunk[0], -FAR)
                for k in range(3, 6):
                    chunk[k] = chunk[k] * friction
                chunk[6] = centred(chunk[6], step_tag) * (1.0 / hash_prime)
                terms = pair_terms(own, chunk, step_tag)
                return tuple(sums[k] + terms[k] for k in range(3))

            sums = lax.fori_loop(0, chunks, one_chunk, (zero, zero, zero))
            folded = [jnp.sum(part, axis=1, keepdims=True) for part in sums]
            force_cols[pl.ds(at, BLOCK), :] = jnp.where(
                lane_block == 0, folded[0], jnp.where(lane_block == 1, folded[1], folded[2])
            )
            return carry

        lax.fori_loop(0, blocks, one_block, 0)
        force = force_cols[...].T[0:3, :]
        force = jnp.where(own_tile[7:8, :] > 0.5, force, 0.0)
        state = state_ref[ix, iy, iz]
        vel, old = state[0:3, :], state[3:6, :]
        new_vel = vel + 0.5 * time_step * (old + force)
        if closing_eval == 2:
            for k in range(3):
                rest[0][k, ix, iy, pl.ds(iz, 1), :] = own_tile[k : k + 1, :]
                rest[1][k, ix, iy, pl.ds(iz, 1), :] = new_vel[k : k + 1, :]
        if closing_eval:
            position = own_tile[0:3, :]
            position = position + time_step * new_vel + 0.5 * time_step * time_step * force
            guessed = new_vel + predict_weight * time_step * force
            state_out[ix, iy, iz, 0:3, :] = new_vel
            state_out[ix, iy, iz, 3:6, :] = force
            state_out[ix, iy, iz, 6:8, :] = own_tile[6:8, :]
            tile_out[ix, iy, iz, 0:3, :] = position
            tile_out[ix, iy, iz, 3:6, :] = guessed
        else:
            state_out[ix, iy, iz] = state
            tile_out[ix, iy, iz, 0:3, :] = own_tile[0:3, :]
            tile_out[ix, iy, iz, 3:6, :] = new_vel
        tile_out[ix, iy, iz, 6:8, :] = own_tile[6:8, :]
        return carry

    lax.fori_loop(0, cells, one_cell, 0)


def force_call(step_tag, closing_eval, cell_count, padded, state):
    px, py, pz = padded.shape[:3]
    cx, cy, cz = state.shape[:3]
    cells = cx * cy * cz
    near = len(NEAR)
    ends = (3, cx, cy, cz, LANES)
    extra = 2 if closing_eval == 2 else 0
    tall = -(-py // 8) * 8
    return pl.pallas_call(
        functools.partial(force_kernel, step_tag, closing_eval),
        out_shape=(
            jax.ShapeDtypeStruct(state.shape, jnp.float32),
            jax.ShapeDtypeStruct(state.shape, jnp.float32),
        )
        + (jax.ShapeDtypeStruct(ends, jnp.float32),) * extra,
        in_specs=[
            pl.BlockSpec(memory_space=pltpu.SMEM),
            pl.BlockSpec(memory_space=pltpu.VMEM),
            pl.BlockSpec(memory_space=pltpu.VMEM),
        ],
        out_specs=(
            pl.BlockSpec(memory_space=pltpu.VMEM),
            pl.BlockSpec(memory_space=pltpu.VMEM),
        )
        + (pl.BlockSpec(memory_space=pltpu.VMEM),) * extra,
        scratch_shapes=[
            pltpu.VMEM((3, px, pz, tall, LANES), jnp.float32),
            pltpu.VMEM((near * cells, LANES), jnp.float32),
            pltpu.VMEM((near * cells, LANES), jnp.int32),
            pltpu.VMEM((cells, LANES), jnp.int32),
            pltpu.SMEM((cells, LANES), jnp.int32),
            pltpu.VMEM((near + 1, ROWS, LANES), jnp.float32),
            pltpu.VMEM((LANES, ROWS), jnp.float32),
            pltpu.VMEM((LANES, LANES), jnp.float32),
            pltpu.SemaphoreType.DMA,
        ],
        compiler_params=pltpu.CompilerParams(vmem_limit_bytes=32 * 1024 * 1024),
        name="pair_forces",
    )(cell_count, padded, state)


MESH = pl.DeviceIdType.MESH
AROUND = [offset for offset in NEAR if offset != (0, 0, 0)]


def when(condition, body):
    if condition is None:
        body()
    else:
        pl.when(condition)(body)


def beside(offset, sizes):
    nx, ny, nz = sizes
    target = (
        lax.rem(lax.axis_index("gx") + (offset[0] + nx), nx),
        lax.axis_index("gy") + offset[1],
        lax.axis_index("gz") + offset[2],
    )
    exists = None
    for step, place, size in ((offset[1], target[1], ny), (offset[2], target[2], nz)):
        if step != 0:
            inside = place >= 0 if step < 0 else place < size
            exists = inside if exists is None else exists & inside
    return target, exists


def source_slice(step, count):
    return pl.ds(0, count) if step == 0 else pl.ds(count - 1 if step > 0 else 0, 1)


def halo_slice(step, count):
    return pl.ds(1, count) if step == 0 else pl.ds(0 if step > 0 else count + 1, 1)


def exchange_body(sizes, fill, source_ref, padded_ref, send_sems, recv_sems):
    extent = tuple(size - 2 for size in padded_ref.shape[:3])
    barrier = pltpu.get_barrier_semaphore()
    places = {offset: beside(offset, sizes) for offset in AROUND}
    for offset in AROUND:
        target, exists = places[offset]

        def greet(target=target):
            pl.semaphore_signal(barrier, inc=1, device_id=target, device_id_type=MESH)

        when(exists, greet)
    fill()
    copies = {}
    for number, offset in enumerate(AROUND):
        target, exists = places[offset]
        back = tuple(-step for step in offset)
        area = tuple(halo_slice(back[k], extent[k]) for k in range(3))
        if exists is not None:

            def blank(area=area):
                shape = tuple(part.size for part in area) + padded_ref.shape[3:]
                padded_ref[area] = jnp.zeros(shape, jnp.float32)

            pl.when(jnp.logical_not(exists))(blank)
        copies[offset] = pltpu.make_async_remote_copy(
            src_ref=source_ref.at[tuple(source_slice(offset[k], extent[k]) for k in range(3))],
            dst_ref=padded_ref.at[tuple(halo_slice(offset[k], extent[k]) for k in range(3))],
            send_sem=send_sems.at[number],
            recv_sem=recv_sems.at[number],
            device_id=target,
            device_id_type=MESH,
        )
    around = 3
    for axis, size in (("gy", sizes[1]), ("gz", sizes[2])):
        place = lax.axis_index(axis)
        around = around * (1 + jnp.minimum(place, 1) + jnp.minimum(size - 1 - place, 1))
    pl.semaphore_wait(barrier, around - 1)
    for offset in AROUND:
        when(places[offset][1], copies[offset].start)
    for offset in AROUND:
        back = tuple(-step for step in offset)
        when(places[back][1], copies[offset].wait_recv)
    for offset in AROUND:
        when(places[offset][1], copies[offset].wait_send)


def exchange_kernel(sizes, tile_ref, padded_ref, send_sems, recv_sems):
    cx, cy, cz = tile_ref.shape[:3]

    def fill():
        padded_ref[1 : 1 + cx, 1 : 1 + cy, 1 : 1 + cz] = tile_ref[...]

    exchange_body(sizes, fill, tile_ref, padded_ref, send_sems, recv_sems)


def first_kernel(
    sizes, count_ref, pos_ref, vel_ref, force_ref, seed_ref, padded_ref, state_ref,
    tile_ref, send_sems, recv_sems,
):
    cx, cy, cz = tile_ref.shape[:3]
    slot = lax.broadcasted_iota(jnp.int32, (1, LANES), 1)

    def fill():
        for ix in range(cx):
            for iy in range(cy):
                for iz in range(cz):
                    pos, vel, force = [
                        ref[:, ix, iy, iz, :] for ref in (pos_ref, vel_ref, force_ref)
                    ]
                    seed = seed_ref[ix, iy, iz : iz + 1, :].astype(jnp.float32)
                    here = jnp.where(slot < count_ref[ix, iy, iz], 1.0, 0.0)
                    pos = pos + time_step * vel + 0.5 * time_step * time_step * force
                    guessed = vel + predict_weight * time_step * force
                    for ref, top, low in ((tile_ref, pos, guessed), (state_ref, vel, force)):
                        ref[ix, iy, iz, 0:3, :] = top
                        ref[ix, iy, iz, 3:6, :] = low
                        ref[ix, iy, iz, 6:7, :] = seed
                        ref[ix, iy, iz, 7:8, :] = here
        padded_ref[1 : 1 + cx, 1 : 1 + cy, 1 : 1 + cz] = tile_ref[...]

    exchange_body(sizes, fill, tile_ref, padded_ref, send_sems, recv_sems)


VMEM_SPEC = pl.BlockSpec(memory_space=pltpu.VMEM)
SMEM_SPEC = pl.BlockSpec(memory_space=pltpu.SMEM)


def mesh_sizes():
    return tuple(lax.axis_size(axis) for axis in ("gx", "gy", "gz"))


def padded_shape(extent):
    return tuple(size + 2 for size in extent) + (ROWS, LANES)


def exchange_sems():
    return [pltpu.SemaphoreType.DMA((len(AROUND),)), pltpu.SemaphoreType.DMA((len(AROUND),))]


def comm_params(number):
    return pltpu.CompilerParams(
        collective_id=number, has_side_effects=True, vmem_limit_bytes=32 * 1024 * 1024
    )


def exchange_call(tile):
    return pl.pallas_call(
        functools.partial(exchange_kernel, mesh_sizes()),
        out_shape=jax.ShapeDtypeStruct(padded_shape(tile.shape[:3]), jnp.float32),
        in_specs=[VMEM_SPEC],
        out_specs=VMEM_SPEC,
        scratch_shapes=exchange_sems(),
        compiler_params=comm_params(1),
        name="exchange",
    )(tile)


def first_call(cell_count, bead_pos, bead_vel, bead_force, pair_seed):
    extent = cell_count.shape
    return pl.pallas_call(
        functools.partial(first_kernel, mesh_sizes()),
        out_shape=(
            jax.ShapeDtypeStruct(padded_shape(extent), jnp.float32),
            jax.ShapeDtypeStruct(extent + (ROWS, LANES), jnp.float32),
        ),
        in_specs=[SMEM_SPEC] + [VMEM_SPEC] * 4,
        out_specs=(VMEM_SPEC, VMEM_SPEC),
        scratch_shapes=[pltpu.VMEM(extent + (ROWS, LANES), jnp.float32)] + exchange_sems(),
        compiler_params=comm_params(2),
        name="first_exchange",
    )(cell_count, bead_pos, bead_vel, bead_force, pair_seed)


def project_kernel(
    sizes, state_ref, half_ref, grid_ref, map_ref, grid_out, pressure_out, brick_out,
    mine, along_z, along_y, slots_z, slots_y, whole, fields, send_sems, recv_sems,
):
    nx, ny, nz = sizes
    cx, cy, cz = state_ref.shape[:3]
    rows, depth = grid_ref.shape[2:]
    span = mine.shape[2]
    count_y = span // depth
    here = (lax.axis_index("gx"), lax.axis_index("gy"), lax.axis_index("gz"))
    barrier = pltpu.get_barrier_semaphore()
    peers = []
    for axis, size in ((2, nz), (1, ny), (0, nx)):
        for step in range(1, size):
            target = list(here)
            target[axis] = lax.rem(here[axis] + step, size)
            peers.append((axis, step, tuple(target)))
    for axis, step, target in peers:
        pl.semaphore_signal(barrier, inc=1, device_id=target, device_id_type=MESH)

    lane = lax.broadcasted_iota(jnp.int32, (ROWS, span), 1)
    row_id = lax.broadcasted_iota(jnp.int32, (ROWS, LANES), 0)
    for ix in range(cx):
        placed = jnp.zeros((ROWS, span), jnp.float32)
        for row in range(rows):
            mine[ix] = jnp.zeros((ROWS, span), jnp.float32)
            for k in range(3):
                mine[ix, 4 + k : 5 + k, 0:depth] = grid_ref[k, ix, row : row + 1, :]
            mine[ix, 7:8, 0:depth] = map_ref[ix, row : row + 1, :].astype(jnp.float32)
            at = ((here[1] * nz + here[2]) * rows + row) * depth
            placed = placed + pltpu.roll(mine[ix], at, 1)
        for iy in range(cy):
            for iz in range(cz):
                tile = state_ref[ix, iy, iz]
                values = jnp.where(row_id < 3, tile, jnp.where(row_id == 3, 1.0, 0.0))
                values = jnp.where(tile[7:8, :] > 0.5, values, 0.0)
                half = half_ref[ix, iy, iz : iz + 1, :]
                for side in (0, 1):
                    total = jnp.sum(
                        jnp.where(half == side, values, 0.0), axis=1, keepdims=True
                    )
                    at = (here[1] * cy + iy) * depth + (here[2] * cz + iz) * 2 + side
                    placed = placed + jnp.where(lane == at, total, 0.0)
        mine[ix] = placed

    pl.semaphore_wait(barrier, len(peers))
    number = 0
    for axis, source, slots, size, result in (
        (2, mine, slots_z, nz, along_z),
        (1, along_z, slots_y, ny, along_y),
        (0, along_y, None, nx, None),
    ):
        copies = []
        for peer_axis, step, target in peers:
            if peer_axis != axis:
                continue
            if axis == 0:
                landing = whole.at[pl.ds(here[0] * cx, cx)]
            else:
                landing = slots.at[step - 1]
            copies.append(
                pltpu.make_async_remote_copy(
                    src_ref=source,
                    dst_ref=landing,
                    send_sem=send_sems.at[number],
                    recv_sem=recv_sems.at[number],
                    device_id=target,
                    device_id_type=MESH,
                )
            )
            number += 1
        for copy in copies:
            copy.start()
        if axis == 0:
            whole[pl.ds(here[0] * cx, cx)] = source[...]
        for copy in copies:
            copy.wait()
        if axis != 0:
            total = source[...]
            for step in range(1, size):
                total = total + slots[step - 1]
            result[...] = total

    parts = [whole[:, k, :] for k in range(8)]
    lanes = lax.broadcasted_iota(jnp.int32, parts[0].shape, 1)
    place_z = lax.rem(lanes, depth)
    place_y = lanes // depth
    count_x = parts[0].shape[0]

    def after(field, axis):
        if axis == 0:
            return pltpu.roll(field, count_x - 1, 0)
        if axis == 1:
            return jnp.where(place_y == count_y - 1, 0.0, pltpu.roll(field, span - depth, 1))
        return jnp.where(place_z == depth - 1, 0.0, pltpu.roll(field, span - 1, 1))

    def prior(field, axis):
        if axis == 0:
            return pltpu.roll(field, 1, 0)
        if axis == 1:
            return jnp.where(place_y == 0, 0.0, pltpu.roll(field, depth, 1))
        return jnp.where(place_z == 0, 0.0, pltpu.roll(field, 1, 1))

    def total_of(field):
        return jnp.sum(jnp.sum(field, axis=0, keepdims=True), axis=1, keepdims=True)

    share = jnp.maximum(parts[3], 1.0)
    coupled = [
        parts[4 + k] + couple_rate * parts[7] * (parts[k] / share - parts[4 + k])
        for k in range(3)
    ]
    divergence = 0.0
    for k in range(3):
        divergence = divergence + after(coupled[k], k) - prior(coupled[k], k)
    residual = -0.5 * divergence
    direction = residual
    pressure = jnp.zeros_like(residual)
    norm_now = total_of(residual * residual)
    for repeat in range(ITERS):
        around = 0.0
        for k in range(3):
            around = around + after(direction, k) + prior(direction, k)
        applied = 6.0 * direction - around
        step_length = norm_now / total_of(direction * applied)
        pressure = pressure + step_length * direction
        residual = residual - step_length * applied
        norm_next = total_of(residual * residual)
        direction = residual + norm_next / norm_now * direction
        norm_now = norm_next
    for k in range(3):
        fields[:, k, :] = coupled[k] - 0.5 * (after(pressure, k) - prior(pressure, k))
    fields[:, 3, :] = pressure
    for ix in range(cx):
        own = fields[here[0] * cx + ix]
        for row in range(rows):
            start = ((here[1] * nz + here[2]) * rows + row) * depth
            band = pltpu.roll(own, lax.rem(span - start, span), 1)
            for k in range(3):
                grid_out[k, ix, row : row + 1, :] = band[k : k + 1, 0:depth]
            pressure_out[ix, row : row + 1, :] = band[3:4, 0:depth]
        for iy in range(cy):
            start = (here[1] * cy + iy) * depth + here[2] * cz * 2
            band = pltpu.roll(own, lax.rem(span - start, span), 1)
            for k in range(3):
                brick_out[k, ix, iy : iy + 1, :] = band[k : k + 1, 0 : cz * 2]


def project_call(state, bead_half, grid_vel, correlation_map):
    sizes = mesh_sizes()
    nx, ny, nz = sizes
    cx, cy, cz = state.shape[:3]
    depth = grid_vel.shape[3]
    span = ny * cy * depth
    shape = (cx, ROWS, span)
    peers = nx + ny + nz - 3
    return pl.pallas_call(
        functools.partial(project_kernel, sizes),
        out_shape=(
            jax.ShapeDtypeStruct(grid_vel.shape, jnp.float32),
            jax.ShapeDtypeStruct(correlation_map.shape, jnp.float32),
            jax.ShapeDtypeStruct((3, cx, cy, cz * 2), jnp.float32),
        ),
        in_specs=[VMEM_SPEC] * 4,
        out_specs=(VMEM_SPEC,) * 3,
        scratch_shapes=[
            pltpu.VMEM(shape, jnp.float32),
            pltpu.VMEM(shape, jnp.float32),
            pltpu.VMEM(shape, jnp.float32),
            pltpu.VMEM((max(nz - 1, 1),) + shape, jnp.float32),
            pltpu.VMEM((max(ny - 1, 1),) + shape, jnp.float32),
            pltpu.VMEM((nx * cx, ROWS, span), jnp.float32),
            pltpu.VMEM((nx * cx, ROWS, span), jnp.float32),
            pltpu.SemaphoreType.DMA((max(peers, 1),)),
            pltpu.SemaphoreType.DMA((max(peers, 1),)),
        ],
        compiler_params=comm_params(3),
        name="project",
    )(state, bead_half, grid_vel, correlation_map)


def per_device(
    bead_pos, bead_vel, bead_force, cell_count, pair_seed, bead_half, grid_vel, correlation_map
):
    padded, state = first_call(cell_count, bead_pos, bead_vel, bead_force, pair_seed)
    for step_number in range(STEPS):
        step_tag = step_number + 3
        if step_number > 0:
            padded = exchange_call(tile)
        tile, state = force_call(step_tag, 0, cell_count, padded, state)
        padded = exchange_call(tile)
        last = 2 if step_number == STEPS - 1 else 1
        tile, state, *ends = force_call(step_tag, last, cell_count, padded, state)
    position, velocity = ends
    return (position, velocity, *project_call(state, bead_half, grid_vel, correlation_map))


def solution(mesh):
    placed = (
        P(None, "gx", "gy", "gz", None),
        P(None, "gx", "gy", "gz", None),
        P(None, "gx", "gy", "gz", None),
        P("gx", "gy", "gz"),
        P("gx", "gy", "gz", None),
        P("gx", "gy", "gz", None),
        P(None, "gx", ("gy", "gz"), None),
        P("gx", ("gy", "gz"), None),
    )
    return jax.shard_map(
        per_device,
        mesh=mesh,
        in_specs=placed,
        out_specs=(
            P(None, "gx", "gy", "gz", None),
            P(None, "gx", "gy", "gz", None),
            P(None, "gx", ("gy", "gz"), None),
            P("gx", ("gy", "gz"), None),
            P(None, "gx", "gy", "gz"),
        ),
        check_vma=False,
    )
```

```python
import functools
import math

import jax
import jax.numpy as jnp
from jax import lax
from jax.experimental import pallas as pl
from jax.experimental.pallas import tpu as pltpu
from jax.sharding import PartitionSpec as P

STEPS = 2
ITERS = 4

cell_edge = 3.0
conserve = 25.0
friction = 4.5
noise_scale = 3.0 * math.sqrt(12.0) / math.sqrt(0.04)
time_step = 0.04
predict_weight = 0.65
couple_rate = 0.5
hash_prime = 4093

LANES = 128
ROWS = 8
BLOCK = 32
FAR = 1.0e15
NEAR = [(ox, oy, oz) for ox in (-1, 0, 1) for oy in (-1, 0, 1) for oz in (-1, 0, 1)]


VMEM_SPEC = pl.BlockSpec(memory_space=pltpu.VMEM)
SMEM_SPEC = pl.BlockSpec(memory_space=pltpu.SMEM)


def pair_terms(own, chunk, step_tag):
    deltas = [own[k] - chunk[k] for k in range(3)]
    square = deltas[0] * deltas[0] + deltas[1] * deltas[1] + deltas[2] * deltas[2]
    weight = jnp.maximum(1.0 - square, 0.0)
    closing = deltas[0] * (own[3] - chunk[3])
    closing = closing + deltas[1] * (own[4] - chunk[4])
    closing = closing + deltas[2] * (own[5] - chunk[5])
    turns = own[6] * chunk[6] + (0.5 - step_tag * step_tag) / hash_prime
    part = turns - jnp.floor(turns)
    steady = part * noise_scale + (conserve - (0.5 + 0.5 / hash_prime) * noise_scale)
    strength = weight * (steady - weight * closing)
    return [strength * deltas[k] for k in range(3)]


def centred(seed, step_tag):
    moved = seed + float(step_tag)
    return jnp.where(moved > 2046.0, moved - float(hash_prime), moved)


def select_beads(padded_ref, rows_x, masks, index_ref, base_ref):
    px, py, pz = padded_ref.shape[:3]
    cx, cy, cz = px - 2, py - 2, pz - 2
    cells = cx * cy * cz
    for ix in range(px):
        for iz in range(pz):
            present = padded_ref[ix, :, iz, 7, :] > 0.5
            for k in range(3):
                rows_x[k, ix, iz, 0:py, :] = jnp.where(present, padded_ref[ix, :, iz, k, :], FAR)

    for ix in range(cx):
        for iz in range(cz):
            row = (ix * cz + iz) * cy
            low, high = [], []
            for k in range(3):
                mine = rows_x[k, 1 + ix, 1 + iz, 1 : 1 + cy, :]
                there = mine < 0.1 * FAR
                least = jnp.min(jnp.where(there, mine, FAR), axis=1, keepdims=True)
                most = jnp.max(jnp.where(there, mine, -FAR), axis=1, keepdims=True)
                low.append(least - 1.001 - 1e-6 * jnp.abs(least))
                high.append(most + 1.001 + 1e-6 * jnp.abs(most))
            for n, offset in enumerate(NEAR):
                keep = None
                for k in range(3):
                    near = rows_x[
                        k, 1 + ix + offset[0], 1 + iz + offset[2], 1 + offset[1] : 1 + offset[1] + cy, :
                    ]
                    shift = cell_edge * offset[k]
                    inside = (near >= low[k] - shift) & (near <= high[k] - shift)
                    keep = inside if keep is None else keep & inside
                masks[n * cells + row : n * cells + row + cy, :] = jnp.where(keep, 1.0, 0.0)

    mask = masks[...]
    before = lax.broadcasted_iota(jnp.int32, (LANES, LANES), 0)
    after = lax.broadcasted_iota(jnp.int32, (LANES, LANES), 1)
    upper = jnp.where(before < after, 1.0, 0.0).astype(jnp.bfloat16)
    ones = jnp.ones((LANES, LANES), jnp.bfloat16)
    mask16 = mask.astype(jnp.bfloat16)
    rank = jnp.dot(mask16, upper, preferred_element_type=jnp.float32).astype(jnp.int32)
    count = jnp.dot(mask16, ones, preferred_element_type=jnp.float32).astype(jnp.int32)
    spot = lax.broadcasted_iota(jnp.int32, mask.shape, 1)
    entry = jnp.where(mask > 0.5, (spot - rank) * LANES + spot, spot)
    for bit in range(7):
        width = 1 << bit
        flag = LANES << bit
        moved = pltpu.roll(entry, LANES - width, 1)
        stay = jnp.where((entry & flag) != 0, entry & (LANES - 1), entry)
        entry = jnp.where((moved & flag) != 0, moved, stay)
    entry = entry & (LANES - 1)
    bases = []
    running = jnp.zeros((cells, LANES), jnp.int32)
    table = jnp.zeros((cells, LANES), jnp.int32)
    spot_cells = lax.broadcasted_iota(jnp.int32, (cells, LANES), 1)
    for n in range(len(NEAR)):
        bases.append(running)
        table = jnp.where(spot_cells == n, running, table)
        running = running + count[n * cells : (n + 1) * cells, :]
    base_ref[...] = jnp.where(spot_cells == len(NEAR), running, table)
    base_all = jnp.concatenate(bases, axis=0)
    for bit in range(7):
        width = 1 << bit
        entry = jnp.where((base_all & width) != 0, pltpu.roll(entry, width, 1), entry)
    index_ref[...] = entry


def force_kernel(step_tag, phase, count_ref, padded_ref, state_ref, *refs):
    if phase == 0:
        tile_out, index_ref, base_ref, *scratch = refs
    elif phase == 1:
        index_ref, base_ref, tile_out, state_out, *scratch = refs
    else:
        index_ref, base_ref, state_out, pos_out, vel_out, *scratch = refs
    rows_x, masks, shifts, base_smem, list_ref, own_wide, force_wide, copy_sem = scratch
    px, py, pz = padded_ref.shape[:3]
    cx, cy, cz = px - 2, py - 2, pz - 2
    cells = cx * cy * cz
    if phase == 0:
        select_beads(padded_ref, rows_x, masks, index_ref, base_ref)
    to_smem = pltpu.make_async_copy(base_ref, base_smem, copy_sem)
    to_smem.start()
    lane = lax.broadcasted_iota(jnp.int32, (ROWS, LANES), 1)
    row_id = lax.broadcasted_iota(jnp.int32, (ROWS, LANES), 0)
    for n, offset in enumerate(NEAR):
        shift = jnp.zeros((ROWS, LANES), jnp.float32)
        for k in range(3):
            shift = jnp.where(row_id == k, cell_edge * offset[k], shift)
        shifts[n] = shift
    eye = lax.broadcasted_iota(jnp.int32, (LANES, LANES), 0) == lax.broadcasted_iota(
        jnp.int32, (LANES, LANES), 1
    )
    zero = jnp.zeros((BLOCK, LANES), jnp.float32)
    to_smem.wait()

    def one_cell(cell, carry):
        ix = cell // (cy * cz)
        iz = (cell // cy) % cz
        iy = cell % cy
        current = jnp.zeros((ROWS, LANES), jnp.float32)
        for n, offset in enumerate(NEAR):
            tile = padded_ref[ix + 1 + offset[0], iy + 1 + offset[1], iz + 1 + offset[2]]
            index = jnp.broadcast_to(index_ref[pl.ds(n * cells + cell, 1), :], (ROWS, LANES))
            found = jnp.take_along_axis(tile, index, axis=1) + shifts[n]
            base = base_smem[cell, n]
            following = base_smem[cell, n + 1]
            merged = jnp.where(lane >= (base & (LANES - 1)), found, current)
            list_ref[base >> 7] = merged
            crossed = (following >> 7) > (base >> 7)
            current = jnp.where(crossed, found, merged)
        total = base_smem[cell, len(NEAR)]
        list_ref[total >> 7] = jnp.where(
            (row_id == 0) & (lane >= (total & (LANES - 1))), -FAR, current
        )
        chunks = (total + LANES - 1) >> 7
        own_tile = padded_ref[ix + 1, iy + 1, iz + 1]
        own_cols = own_tile.T
        for k in range(7):
            own_wide[k] = jnp.broadcast_to(own_cols[:, k : k + 1], (LANES, LANES))
        blocks = (count_ref[ix, iy, iz] + BLOCK - 1) // BLOCK

        def one_block(block, carry):
            at = pl.multiple_of(block * BLOCK, BLOCK)
            own = [own_wide[k, pl.ds(at, BLOCK), :] for k in range(7)]
            own[6] = own[6] * (1.0 / hash_prime)

            def one_chunk(index, sums):
                chunk = [list_ref[index, k : k + 1, :] for k in range(7)]
                terms = pair_terms(own, chunk, step_tag)
                return tuple(sums[k] + terms[k] for k in range(3))

            sums = lax.fori_loop(0, chunks, one_chunk, (zero, zero, zero))
            for k in range(3):
                force_wide[k, pl.ds(at, BLOCK), :] = sums[k]
            return carry

        lax.fori_loop(0, blocks, one_block, 0)
        state = state_ref[ix, iy, iz]
        new_vel, force = [], []
        for k in range(3):
            column = jnp.sum(force_wide[k], axis=1, keepdims=True)
            row = jnp.sum(jnp.where(eye, column, 0.0), axis=0, keepdims=True)
            row = jnp.where(own_tile[7:8, :] > 0.5, row, 0.0)
            force.append(row)
            new_vel.append(
                state[k : k + 1, :] + 0.5 * time_step * (state[3 + k : 4 + k, :] + row)
            )
        if phase == 0:
            for k in range(3):
                tile_out[ix, iy, iz, k : k + 1, :] = own_tile[k : k + 1, :]
                tile_out[ix, iy, iz, 3 + k : 4 + k, :] = friction * new_vel[k]
            tile_out[ix, iy, iz, 6:8, :] = own_tile[6:8, :]
            return carry
        for k in range(3):
            state_out[ix, iy, iz, k : k + 1, :] = new_vel[k]
            state_out[ix, iy, iz, 3 + k : 4 + k, :] = force[k]
        state_out[ix, iy, iz, 6:8, :] = state[6:8, :]
        for k in range(3):
            position = own_tile[k : k + 1, :]
            if phase == 2:
                pos_out[k, ix, iy, pl.ds(iz, 1), :] = position
                vel_out[k, ix, iy, pl.ds(iz, 1), :] = new_vel[k]
                continue
            position = position + time_step * new_vel[k]
            position = position + 0.5 * time_step * time_step * force[k]
            tile_out[ix, iy, iz, k : k + 1, :] = position
            guessed = new_vel[k] + predict_weight * time_step * force[k]
            tile_out[ix, iy, iz, 3 + k : 4 + k, :] = friction * guessed
        if phase == 1:
            tile_out[ix, iy, iz, 6:7, :] = centred(state[6:7, :], step_tag + 1)
            tile_out[ix, iy, iz, 7:8, :] = state[7:8, :]
        return carry

    lax.fori_loop(0, cells, one_cell, 0)


def force_call(step_tag, phase, cell_count, padded, state, *selection):
    px, py, pz = padded.shape[:3]
    cx, cy, cz = state.shape[:3]
    cells = cx * cy * cz
    near = len(NEAR)
    tall = -(-py // 8) * 8
    brick = jax.ShapeDtypeStruct(state.shape, jnp.float32)
    beads = jax.ShapeDtypeStruct((3, cx, cy, cz, LANES), jnp.float32)
    if phase == 0:
        index = jax.ShapeDtypeStruct((near * cells, LANES), jnp.int32)
        outs = (brick, index, jax.ShapeDtypeStruct((cells, LANES), jnp.int32))
    else:
        outs = (brick, brick) if phase == 1 else (brick, beads, beads)
    return pl.pallas_call(
        functools.partial(force_kernel, step_tag, phase),
        out_shape=outs,
        in_specs=[SMEM_SPEC] + [VMEM_SPEC] * (2 + len(selection)),
        out_specs=(VMEM_SPEC,) * len(outs),
        scratch_shapes=[
            pltpu.VMEM((3, px, pz, tall, LANES), jnp.float32),
            pltpu.VMEM((near * cells, LANES), jnp.float32),
            pltpu.VMEM((near, ROWS, LANES), jnp.float32),
            pltpu.SMEM((cells, LANES), jnp.int32),
            pltpu.VMEM((near + 1, ROWS, LANES), jnp.float32),
            pltpu.VMEM((7, LANES, LANES), jnp.float32),
            pltpu.VMEM((3, LANES, LANES), jnp.float32),
            pltpu.SemaphoreType.DMA,
        ],
        compiler_params=pltpu.CompilerParams(vmem_limit_bytes=32 * 1024 * 1024),
        name="pair_forces",
    )(cell_count, padded, state, *selection)


MESH = pl.DeviceIdType.MESH
AROUND = [offset for offset in NEAR if offset != (0, 0, 0)]


def when(condition, body):
    if condition is None:
        body()
    else:
        pl.when(condition)(body)


def beside(offset, sizes):
    nx, ny, nz = sizes
    target = (
        lax.rem(lax.axis_index("gx") + (offset[0] + nx), nx),
        lax.axis_index("gy") + offset[1],
        lax.axis_index("gz") + offset[2],
    )
    exists = None
    for step, place, size in ((offset[1], target[1], ny), (offset[2], target[2], nz)):
        if step != 0:
            inside = place >= 0 if step < 0 else place < size
            exists = inside if exists is None else exists & inside
    return target, exists


def source_slice(step, count):
    return pl.ds(0, count) if step == 0 else pl.ds(count - 1 if step > 0 else 0, 1)


def halo_slice(step, count):
    return pl.ds(1, count) if step == 0 else pl.ds(0 if step > 0 else count + 1, 1)


def exchange_body(sizes, fill, source_ref, padded_ref, send_sems, recv_sems):
    extent = tuple(size - 2 for size in padded_ref.shape[:3])
    barrier = pltpu.get_barrier_semaphore()
    places = {offset: beside(offset, sizes) for offset in AROUND}
    for offset in AROUND:
        target, exists = places[offset]

        def greet(target=target):
            pl.semaphore_signal(barrier, inc=1, device_id=target, device_id_type=MESH)

        when(exists, greet)
    fill()
    copies = {}
    for number, offset in enumerate(AROUND):
        target, exists = places[offset]
        back = tuple(-step for step in offset)
        area = tuple(halo_slice(back[k], extent[k]) for k in range(3))
        if exists is not None:

            def blank(area=area):
                shape = tuple(part.size for part in area) + padded_ref.shape[3:]
                padded_ref[area] = jnp.zeros(shape, jnp.float32)

            pl.when(jnp.logical_not(exists))(blank)
        copies[offset] = pltpu.make_async_remote_copy(
            src_ref=source_ref.at[tuple(source_slice(offset[k], extent[k]) for k in range(3))],
            dst_ref=padded_ref.at[tuple(halo_slice(offset[k], extent[k]) for k in range(3))],
            send_sem=send_sems.at[number],
            recv_sem=recv_sems.at[number],
            device_id=target,
            device_id_type=MESH,
        )
    around = 3
    for axis, size in (("gy", sizes[1]), ("gz", sizes[2])):
        place = lax.axis_index(axis)
        around = around * (1 + jnp.minimum(place, 1) + jnp.minimum(size - 1 - place, 1))
    pl.semaphore_wait(barrier, around - 1)
    for offset in AROUND:
        when(places[offset][1], copies[offset].start)
    for offset in AROUND:
        back = tuple(-step for step in offset)
        when(places[back][1], copies[offset].wait_recv)
    for offset in AROUND:
        when(places[offset][1], copies[offset].wait_send)


def exchange_kernel(sizes, tile_ref, padded_ref, send_sems, recv_sems):
    cx, cy, cz = tile_ref.shape[:3]

    def fill():
        padded_ref[1 : 1 + cx, 1 : 1 + cy, 1 : 1 + cz] = tile_ref[...]

    exchange_body(sizes, fill, tile_ref, padded_ref, send_sems, recv_sems)


def first_kernel(
    sizes, count_ref, pos_ref, vel_ref, force_ref, seed_ref, padded_ref, state_ref,
    tile_ref, send_sems, recv_sems,
):
    cx, cy, cz = tile_ref.shape[:3]
    slot = lax.broadcasted_iota(jnp.int32, (1, LANES), 1)

    def fill():
        for ix in range(cx):
            for iy in range(cy):
                for iz in range(cz):
                    pos, vel, force = [
                        ref[:, ix, iy, iz, :] for ref in (pos_ref, vel_ref, force_ref)
                    ]
                    seed = seed_ref[ix, iy, iz : iz + 1, :].astype(jnp.float32)
                    here = jnp.where(slot < count_ref[ix, iy, iz], 1.0, 0.0)
                    pos = pos + time_step * vel + 0.5 * time_step * time_step * force
                    guessed = vel + predict_weight * time_step * force
                    for ref, top, low, mark in (
                        (tile_ref, pos, friction * guessed, centred(seed, 3)),
                        (state_ref, vel, force, seed),
                    ):
                        ref[ix, iy, iz, 0:3, :] = top
                        ref[ix, iy, iz, 3:6, :] = low
                        ref[ix, iy, iz, 6:7, :] = mark
                        ref[ix, iy, iz, 7:8, :] = here
        padded_ref[1 : 1 + cx, 1 : 1 + cy, 1 : 1 + cz] = tile_ref[...]

    exchange_body(sizes, fill, tile_ref, padded_ref, send_sems, recv_sems)


def mesh_sizes():
    return tuple(lax.axis_size(axis) for axis in ("gx", "gy", "gz"))


def padded_shape(extent):
    return tuple(size + 2 for size in extent) + (ROWS, LANES)


def exchange_sems():
    return [pltpu.SemaphoreType.DMA((len(AROUND),)), pltpu.SemaphoreType.DMA((len(AROUND),))]


def comm_params(number):
    return pltpu.CompilerParams(
        collective_id=number, has_side_effects=True, vmem_limit_bytes=32 * 1024 * 1024
    )


def exchange_call(tile):
    return pl.pallas_call(
        functools.partial(exchange_kernel, mesh_sizes()),
        out_shape=jax.ShapeDtypeStruct(padded_shape(tile.shape[:3]), jnp.float32),
        in_specs=[VMEM_SPEC],
        out_specs=VMEM_SPEC,
        scratch_shapes=exchange_sems(),
        compiler_params=comm_params(1),
        name="exchange",
    )(tile)


def first_call(cell_count, bead_pos, bead_vel, bead_force, pair_seed):
    extent = cell_count.shape
    return pl.pallas_call(
        functools.partial(first_kernel, mesh_sizes()),
        out_shape=(
            jax.ShapeDtypeStruct(padded_shape(extent), jnp.float32),
            jax.ShapeDtypeStruct(extent + (ROWS, LANES), jnp.float32),
        ),
        in_specs=[SMEM_SPEC] + [VMEM_SPEC] * 4,
        out_specs=(VMEM_SPEC, VMEM_SPEC),
        scratch_shapes=[pltpu.VMEM(extent + (ROWS, LANES), jnp.float32)] + exchange_sems(),
        compiler_params=comm_params(2),
        name="first_exchange",
    )(cell_count, bead_pos, bead_vel, bead_force, pair_seed)


def gather_kernel(
    sizes, state_ref, half_ref, grid_ref, map_ref, whole,
    mine, along_z, along_y, slots_z, slots_y, send_sems, recv_sems,
):
    nx, ny, nz = sizes
    cx, cy, cz = state_ref.shape[:3]
    rows, depth = grid_ref.shape[2:]
    span = mine.shape[2]
    count_y = span // depth
    here = (lax.axis_index("gx"), lax.axis_index("gy"), lax.axis_index("gz"))
    barrier = pltpu.get_barrier_semaphore()
    peers = []
    for axis, size in ((2, nz), (1, ny), (0, nx)):
        for step in range(1, size):
            target = list(here)
            target[axis] = lax.rem(here[axis] + step, size)
            peers.append((axis, step, tuple(target)))
    for axis, step, target in peers:
        pl.semaphore_signal(barrier, inc=1, device_id=target, device_id_type=MESH)

    lane = lax.broadcasted_iota(jnp.int32, (ROWS, span), 1)
    row_id = lax.broadcasted_iota(jnp.int32, (ROWS, LANES), 0)
    for ix in range(cx):
        placed = jnp.zeros((ROWS, span), jnp.float32)
        for row in range(rows):
            mine[ix] = jnp.zeros((ROWS, span), jnp.float32)
            for k in range(3):
                mine[ix, 4 + k : 5 + k, 0:depth] = grid_ref[k, ix, row : row + 1, :]
            mine[ix, 7:8, 0:depth] = map_ref[ix, row : row + 1, :].astype(jnp.float32)
            at = ((here[1] * nz + here[2]) * rows + row) * depth
            placed = placed + pltpu.roll(mine[ix], at, 1)
        for iy in range(cy):
            for iz in range(cz):
                tile = state_ref[ix, iy, iz]
                values = jnp.where(row_id < 3, tile, jnp.where(row_id == 3, 1.0, 0.0))
                values = jnp.where(tile[7:8, :] > 0.5, values, 0.0)
                half = half_ref[ix, iy, iz : iz + 1, :]
                for side in (0, 1):
                    total = jnp.sum(
                        jnp.where(half == side, values, 0.0), axis=1, keepdims=True
                    )
                    at = (here[1] * cy + iy) * depth + (here[2] * cz + iz) * 2 + side
                    placed = placed + jnp.where(lane == at, total, 0.0)
        mine[ix] = placed

    pl.semaphore_wait(barrier, len(peers))
    number = 0
    for axis, source, slots, size, result in (
        (2, mine, slots_z, nz, along_z),
        (1, along_z, slots_y, ny, along_y),
        (0, along_y, None, nx, None),
    ):
        copies = []
        for peer_axis, step, target in peers:
            if peer_axis != axis:
                continue
            if axis == 0:
                landing = whole.at[pl.ds(here[0] * cx, cx)]
            else:
                landing = slots.at[step - 1]
            copies.append(
                pltpu.make_async_remote_copy(
                    src_ref=source,
                    dst_ref=landing,
                    send_sem=send_sems.at[number],
                    recv_sem=recv_sems.at[number],
                    device_id=target,
                    device_id_type=MESH,
                )
            )
            number += 1
        for copy in copies:
            copy.start()
        if axis == 0:
            whole[pl.ds(here[0] * cx, cx)] = source[...]
        for copy in copies:
            copy.wait()
        if axis != 0:
            total = source[...]
            for step in range(1, size):
                total = total + slots[step - 1]
            result[...] = total


def project_kernel(sizes, extent, rows, depth, whole, grid_out, pressure_out, brick_out, fields):
    nx, ny, nz = sizes
    cx, cy, cz = extent
    span = whole.shape[2]
    count_y = span // depth
    here = (lax.axis_index("gx"), lax.axis_index("gy"), lax.axis_index("gz"))
    parts = [whole[:, k, :] for k in range(8)]
    lanes = lax.broadcasted_iota(jnp.int32, parts[0].shape, 1)
    place_z = lax.rem(lanes, depth)
    place_y = lanes // depth
    count_x = parts[0].shape[0]

    def after(field, axis):
        if axis == 0:
            return pltpu.roll(field, count_x - 1, 0)
        if axis == 1:
            return jnp.where(place_y == count_y - 1, 0.0, pltpu.roll(field, span - depth, 1))
        return jnp.where(place_z == depth - 1, 0.0, pltpu.roll(field, span - 1, 1))

    def prior(field, axis):
        if axis == 0:
            return pltpu.roll(field, 1, 0)
        if axis == 1:
            return jnp.where(place_y == 0, 0.0, pltpu.roll(field, depth, 1))
        return jnp.where(place_z == 0, 0.0, pltpu.roll(field, 1, 1))

    def total_of(field):
        return jnp.sum(jnp.sum(field, axis=0, keepdims=True), axis=1, keepdims=True)

    share = jnp.maximum(parts[3], 1.0)
    coupled = [
        parts[4 + k] + couple_rate * parts[7] * (parts[k] / share - parts[4 + k])
        for k in range(3)
    ]
    divergence = 0.0
    for k in range(3):
        divergence = divergence + after(coupled[k], k) - prior(coupled[k], k)
    residual = -0.5 * divergence
    direction = residual
    pressure = jnp.zeros_like(residual)
    norm_now = total_of(residual * residual)
    for repeat in range(ITERS):
        around = 0.0
        for k in range(3):
            around = around + after(direction, k) + prior(direction, k)
        applied = 6.0 * direction - around
        step_length = norm_now / total_of(direction * applied)
        pressure = pressure + step_length * direction
        residual = residual - step_length * applied
        norm_next = total_of(residual * residual)
        direction = residual + norm_next / norm_now * direction
        norm_now = norm_next
    for k in range(3):
        fields[:, k, :] = coupled[k] - 0.5 * (after(pressure, k) - prior(pressure, k))
    fields[:, 3, :] = pressure
    for ix in range(cx):
        own = fields[here[0] * cx + ix]
        for row in range(rows):
            start = ((here[1] * nz + here[2]) * rows + row) * depth
            band = pltpu.roll(own, lax.rem(span - start, span), 1)
            for k in range(3):
                grid_out[k, ix, row : row + 1, :] = band[k : k + 1, 0:depth]
            pressure_out[ix, row : row + 1, :] = band[3:4, 0:depth]
        for iy in range(cy):
            start = (here[1] * cy + iy) * depth + here[2] * cz * 2
            band = pltpu.roll(own, lax.rem(span - start, span), 1)
            for k in range(3):
                brick_out[k, ix, iy : iy + 1, :] = band[k : k + 1, 0 : cz * 2]


def project_call(state, bead_half, grid_vel, correlation_map):
    sizes = mesh_sizes()
    nx, ny, nz = sizes
    cx, cy, cz = state.shape[:3]
    depth = grid_vel.shape[3]
    span = ny * cy * depth
    shape = (cx, ROWS, span)
    peers = nx + ny + nz - 3
    whole = jax.ShapeDtypeStruct((nx * cx, ROWS, span), jnp.float32)
    gathered = pl.pallas_call(
        functools.partial(gather_kernel, sizes),
        out_shape=whole,
        in_specs=[VMEM_SPEC] * 4,
        out_specs=VMEM_SPEC,
        scratch_shapes=[
            pltpu.VMEM(shape, jnp.float32),
            pltpu.VMEM(shape, jnp.float32),
            pltpu.VMEM(shape, jnp.float32),
            pltpu.VMEM((max(nz - 1, 1),) + shape, jnp.float32),
            pltpu.VMEM((max(ny - 1, 1),) + shape, jnp.float32),
            pltpu.SemaphoreType.DMA((max(peers, 1),)),
            pltpu.SemaphoreType.DMA((max(peers, 1),)),
        ],
        compiler_params=comm_params(3),
        name="gather_grid",
    )(state, bead_half, grid_vel, correlation_map)
    return pl.pallas_call(
        functools.partial(project_kernel, sizes, (cx, cy, cz), grid_vel.shape[2], depth),
        out_shape=(
            jax.ShapeDtypeStruct(grid_vel.shape, jnp.float32),
            jax.ShapeDtypeStruct(correlation_map.shape, jnp.float32),
            jax.ShapeDtypeStruct((3, cx, cy, cz * 2), jnp.float32),
        ),
        in_specs=[VMEM_SPEC],
        out_specs=(VMEM_SPEC,) * 3,
        scratch_shapes=[pltpu.VMEM(whole.shape, jnp.float32)],
        compiler_params=pltpu.CompilerParams(vmem_limit_bytes=32 * 1024 * 1024),
        name="project",
    )(gathered)


def per_device(
    bead_pos, bead_vel, bead_force, cell_count, pair_seed, bead_half, grid_vel, correlation_map
):
    padded, state = first_call(cell_count, bead_pos, bead_vel, bead_force, pair_seed)
    for step_number in range(STEPS):
        step_tag = step_number + 3
        if step_number > 0:
            padded = exchange_call(tile)
        tile, *selection = force_call(step_tag, 0, cell_count, padded, state)
        padded = exchange_call(tile)
        if step_number < STEPS - 1:
            tile, state = force_call(step_tag, 1, cell_count, padded, state, *selection)
    state, position, velocity = force_call(step_tag, 2, cell_count, padded, state, *selection)
    return (position, velocity, *project_call(state, bead_half, grid_vel, correlation_map))


def solution(mesh):
    placed = (
        P(None, "gx", "gy", "gz", None),
        P(None, "gx", "gy", "gz", None),
        P(None, "gx", "gy", "gz", None),
        P("gx", "gy", "gz"),
        P("gx", "gy", "gz", None),
        P("gx", "gy", "gz", None),
        P(None, "gx", ("gy", "gz"), None),
        P("gx", ("gy", "gz"), None),
    )
    return jax.shard_map(
        per_device,
        mesh=mesh,
        in_specs=placed,
        out_specs=(
            P(None, "gx", "gy", "gz", None),
            P(None, "gx", "gy", "gz", None),
            P(None, "gx", ("gy", "gz"), None),
            P("gx", ("gy", "gz"), None),
            P(None, "gx", "gy", "gz"),
        ),
        check_vma=False,
    )
```

```python
import functools
import math

import jax
import jax.numpy as jnp
from jax import lax
from jax.experimental import pallas as pl
from jax.experimental.pallas import tpu as pltpu
from jax.sharding import PartitionSpec as P

STEPS = 2
ITERS = 4

cell_edge = 3.0
conserve = 25.0
friction = 4.5
noise_scale = 3.0 * math.sqrt(12.0) / math.sqrt(0.04)
time_step = 0.04
predict_weight = 0.65
couple_rate = 0.5
hash_prime = 4093

LANES = 128
ROWS = 8
BLOCK = 32
FAR = 1.0e15
NEAR = [(ox, oy, oz) for ox in (-1, 0, 1) for oy in (-1, 0, 1) for oz in (-1, 0, 1)]


VMEM_SPEC = pl.BlockSpec(memory_space=pltpu.VMEM)
HBM_SPEC = pl.BlockSpec(memory_space=pltpu.HBM)


def pair_terms(own, chunk, step_tag):
    deltas = [own[k] - chunk[k] for k in range(3)]
    square = deltas[0] * deltas[0] + deltas[1] * deltas[1] + deltas[2] * deltas[2]
    weight = jnp.maximum(1.0 - square, 0.0)
    closing = deltas[0] * (own[3] - chunk[3])
    closing = closing + deltas[1] * (own[4] - chunk[4])
    closing = closing + deltas[2] * (own[5] - chunk[5])
    turns = own[6] * chunk[6] + (0.5 - step_tag * step_tag) / hash_prime
    part = turns - jnp.floor(turns)
    steady = part * noise_scale + (conserve - (0.5 + 0.5 / hash_prime) * noise_scale)
    strength = weight * (steady - weight * closing)
    return [strength * deltas[k] for k in range(3)]


def centred(seed, step_tag):
    moved = seed + float(step_tag)
    return jnp.where(moved > 2046.0, moved - float(hash_prime), moved)


def select_beads(padded_ref, rows_x, masks, index_ref, base_ref):
    px, py, pz = padded_ref.shape[:3]
    cx, cy, cz = px - 2, py - 2, pz - 2
    cells = cx * cy * cz
    for ix in range(px):
        for iz in range(pz):
            present = padded_ref[ix, :, iz, 7, :] > 0.5
            for k in range(3):
                rows_x[k, ix, iz, 0:py, :] = jnp.where(present, padded_ref[ix, :, iz, k, :], FAR)

    for ix in range(cx):
        for iz in range(cz):
            row = (ix * cz + iz) * cy
            low, high = [], []
            for k in range(3):
                mine = rows_x[k, 1 + ix, 1 + iz, 1 : 1 + cy, :]
                there = mine < 0.1 * FAR
                if k == 0:
                    held = jnp.sum(jnp.where(there, 1.0, 0.0), axis=1, keepdims=True)
                least = jnp.min(jnp.where(there, mine, FAR), axis=1, keepdims=True)
                most = jnp.max(jnp.where(there, mine, -FAR), axis=1, keepdims=True)
                low.append(least - 1.001 - 1e-6 * jnp.abs(least))
                high.append(most + 1.001 + 1e-6 * jnp.abs(most))
            base_ref[row : row + cy, :] = jnp.broadcast_to(held, (cy, LANES)).astype(jnp.int32)
            for n, offset in enumerate(NEAR):
                keep = None
                for k in range(3):
                    near = rows_x[
                        k, 1 + ix + offset[0], 1 + iz + offset[2], 1 + offset[1] : 1 + offset[1] + cy, :
                    ]
                    shift = cell_edge * offset[k]
                    inside = (near >= low[k] - shift) & (near <= high[k] - shift)
                    keep = inside if keep is None else keep & inside
                masks[n * cells + row : n * cells + row + cy, :] = jnp.where(keep, 1.0, 0.0)

    mask = masks[...]
    before = lax.broadcasted_iota(jnp.int32, (LANES, LANES), 0)
    after = lax.broadcasted_iota(jnp.int32, (LANES, LANES), 1)
    upper = jnp.where(before < after, 1.0, 0.0).astype(jnp.bfloat16)
    ones = jnp.ones((LANES, LANES), jnp.bfloat16)
    mask16 = mask.astype(jnp.bfloat16)
    rank = jnp.dot(mask16, upper, preferred_element_type=jnp.float32).astype(jnp.int32)
    count = jnp.dot(mask16, ones, preferred_element_type=jnp.float32).astype(jnp.int32)
    spot = lax.broadcasted_iota(jnp.int32, mask.shape, 1)
    entry = jnp.where(mask > 0.5, (spot - rank) * LANES + spot, spot)
    for bit in range(7):
        width = 1 << bit
        flag = LANES << bit
        moved = pltpu.roll(entry, LANES - width, 1)
        stay = jnp.where((entry & flag) != 0, entry & (LANES - 1), entry)
        entry = jnp.where((moved & flag) != 0, moved, stay)
    entry = entry & (LANES - 1)
    bases = []
    running = jnp.zeros((cells, LANES), jnp.int32)
    table = base_ref[...]
    spot_cells = lax.broadcasted_iota(jnp.int32, (cells, LANES), 1)
    for n in range(len(NEAR)):
        bases.append(running)
        table = jnp.where(spot_cells == n, running, table)
        running = running + count[n * cells : (n + 1) * cells, :]
    base_ref[...] = jnp.where(spot_cells == len(NEAR), running, table)
    base_all = jnp.concatenate(bases, axis=0)
    for bit in range(7):
        width = 1 << bit
        entry = jnp.where((base_all & width) != 0, pltpu.roll(entry, width, 1), entry)
    index_ref[...] = entry


def force_kernel(step_tag, phase, padded_ref, state_ref, *refs):
    if phase == 0:
        tile_out, index_ref, base_ref, *scratch = refs
    elif phase == 1:
        index_ref, base_ref, tile_out, state_out, *scratch = refs
    else:
        index_ref, base_ref, state_out, pos_out, vel_out, *scratch = refs
    rows_x, masks, shifts, base_smem, list_ref, own_wide, force_wide, copy_sem = scratch
    px, py, pz = padded_ref.shape[:3]
    cx, cy, cz = px - 2, py - 2, pz - 2
    cells = cx * cy * cz
    if phase == 0:
        select_beads(padded_ref, rows_x, masks, index_ref, base_ref)
    to_smem = pltpu.make_async_copy(base_ref, base_smem, copy_sem)
    to_smem.start()
    lane = lax.broadcasted_iota(jnp.int32, (ROWS, LANES), 1)
    row_id = lax.broadcasted_iota(jnp.int32, (ROWS, LANES), 0)
    for n, offset in enumerate(NEAR):
        shift = jnp.zeros((ROWS, LANES), jnp.float32)
        for k in range(3):
            shift = jnp.where(row_id == k, cell_edge * offset[k], shift)
        shifts[n] = shift
    force_wide[...] = jnp.zeros(force_wide.shape, jnp.float32)
    zero = jnp.zeros((BLOCK, LANES), jnp.float32)
    to_smem.wait()

    def place(cell):
        return cell // (cy * cz), cell % cy, (cell // cy) % cz

    def prepare(cell, slot):
        ix, iy, iz = place(cell)
        current = jnp.zeros((ROWS, LANES), jnp.float32)
        for n, offset in enumerate(NEAR):
            tile = padded_ref[ix + 1 + offset[0], iy + 1 + offset[1], iz + 1 + offset[2]]
            index = jnp.broadcast_to(index_ref[pl.ds(n * cells + cell, 1), :], (ROWS, LANES))
            found = jnp.take_along_axis(tile, index, axis=1) + shifts[n]
            base = base_smem[cell, n]
            following = base_smem[cell, n + 1]
            merged = jnp.where(lane >= (base & (LANES - 1)), found, current)
            list_ref[slot, base >> 7] = merged
            crossed = (following >> 7) > (base >> 7)
            current = jnp.where(crossed, found, merged)
        total = base_smem[cell, len(NEAR)]
        list_ref[slot, total >> 7] = jnp.where(
            (row_id == 0) & (lane >= (total & (LANES - 1))), -FAR, current
        )
        own_cols = padded_ref[ix + 1, iy + 1, iz + 1].T
        for k in range(7):
            own_wide[slot, k] = jnp.broadcast_to(own_cols[:, k : k + 1], (LANES, LANES))

    prepare(0, 0)

    def one_cell(cell, carry):
        ix, iy, iz = place(cell)
        slot = cell & 1
        chunks = (base_smem[cell, len(NEAR)] + LANES - 1) >> 7
        blocks = (base_smem[cell, len(NEAR) + 1] + BLOCK - 1) // BLOCK

        def one_block(block, carry):
            at = pl.multiple_of(block * BLOCK, BLOCK)
            own = [own_wide[slot, k, pl.ds(at, BLOCK), :] for k in range(7)]
            own[6] = own[6] * (1.0 / hash_prime)

            def one_chunk(index, sums):
                chunk = [list_ref[slot, index, k : k + 1, :] for k in range(7)]
                terms = pair_terms(own, chunk, step_tag)
                return tuple(sums[k] + terms[k] for k in range(3))

            sums = lax.fori_loop(0, chunks, one_chunk, (zero, zero, zero))
            for k in range(3):
                force_wide[k, pl.ds(at, BLOCK), :] = sums[k]
            return carry

        lax.fori_loop(0, blocks, one_block, 0)
        prepare(jnp.minimum(cell + 1, cells - 1), 1 - slot)
        own_tile = padded_ref[ix + 1, iy + 1, iz + 1]
        wide = force_wide[...].reshape(3 * LANES, LANES)
        coarse = wide.astype(jnp.bfloat16)
        fine = (wide - coarse.astype(jnp.float32)).astype(jnp.bfloat16)
        summed = lax.dot_general(
            jnp.ones((ROWS, 2 * LANES), jnp.bfloat16),
            jnp.concatenate([coarse, fine], axis=1),
            (((1,), (1,)), ((), ())),
            preferred_element_type=jnp.float32,
        )
        state = state_ref[ix, iy, iz]
        new_vel, force = [], []
        for k in range(3):
            row = summed[0:1, k * LANES : (k + 1) * LANES]
            row = jnp.where(own_tile[7:8, :] > 0.5, row, 0.0)
            force.append(row)
            new_vel.append(
                state[k : k + 1, :] + 0.5 * time_step * (state[3 + k : 4 + k, :] + row)
            )
        if phase == 0:
            for k in range(3):
                tile_out[ix, iy, iz, k : k + 1, :] = own_tile[k : k + 1, :]
                tile_out[ix, iy, iz, 3 + k : 4 + k, :] = friction * new_vel[k]
            tile_out[ix, iy, iz, 6:8, :] = own_tile[6:8, :]
            return carry
        for k in range(3):
            state_out[ix, iy, iz, k : k + 1, :] = new_vel[k]
            state_out[ix, iy, iz, 3 + k : 4 + k, :] = force[k]
        state_out[ix, iy, iz, 6:8, :] = state[6:8, :]
        for k in range(3):
            position = own_tile[k : k + 1, :]
            if phase == 2:
                pos_out[k, ix, iy, pl.ds(iz, 1), :] = position
                vel_out[k, ix, iy, pl.ds(iz, 1), :] = new_vel[k]
                continue
            position = position + time_step * new_vel[k]
            position = position + 0.5 * time_step * time_step * force[k]
            tile_out[ix, iy, iz, k : k + 1, :] = position
            guessed = new_vel[k] + predict_weight * time_step * force[k]
            tile_out[ix, iy, iz, 3 + k : 4 + k, :] = friction * guessed
        if phase == 1:
            tile_out[ix, iy, iz, 6:7, :] = centred(state[6:7, :], step_tag + 1)
            tile_out[ix, iy, iz, 7:8, :] = state[7:8, :]
        return carry

    lax.fori_loop(0, cells, one_cell, 0)


def force_call(step_tag, phase, padded, state, *selection):
    px, py, pz = padded.shape[:3]
    cx, cy, cz = state.shape[:3]
    cells = cx * cy * cz
    near = len(NEAR)
    tall = -(-py // 8) * 8
    brick = jax.ShapeDtypeStruct(state.shape, jnp.float32)
    beads = jax.ShapeDtypeStruct((3, cx, cy, cz, LANES), jnp.float32)
    if phase == 0:
        index = jax.ShapeDtypeStruct((near * cells, LANES), jnp.int32)
        outs = (brick, index, jax.ShapeDtypeStruct((cells, LANES), jnp.int32))
    else:
        outs = (brick, brick) if phase == 1 else (brick, beads, beads)
    return pl.pallas_call(
        functools.partial(force_kernel, step_tag, phase),
        out_shape=outs,
        in_specs=[VMEM_SPEC] * (2 + len(selection)),
        out_specs=(VMEM_SPEC,) * len(outs),
        scratch_shapes=[
            pltpu.VMEM((3, px, pz, tall, LANES), jnp.float32),
            pltpu.VMEM((near * cells, LANES), jnp.float32),
            pltpu.VMEM((near, ROWS, LANES), jnp.float32),
            pltpu.SMEM((cells, LANES), jnp.int32),
            pltpu.VMEM((2, near + 1, ROWS, LANES), jnp.float32),
            pltpu.VMEM((2, 7, LANES, LANES), jnp.float32),
            pltpu.VMEM((3, LANES, LANES), jnp.float32),
            pltpu.SemaphoreType.DMA,
        ],
        compiler_params=pltpu.CompilerParams(vmem_limit_bytes=32 * 1024 * 1024),
        name="pair_forces",
    )(padded, state, *selection)


MESH = pl.DeviceIdType.MESH
AROUND = [offset for offset in NEAR if offset != (0, 0, 0)]


def when(condition, body):
    if condition is None:
        body()
    else:
        pl.when(condition)(body)


def beside(offset, sizes):
    nx, ny, nz = sizes
    target = (
        lax.rem(lax.axis_index("gx") + (offset[0] + nx), nx),
        lax.axis_index("gy") + offset[1],
        lax.axis_index("gz") + offset[2],
    )
    exists = None
    for step, place, size in ((offset[1], target[1], ny), (offset[2], target[2], nz)):
        if step != 0:
            inside = place >= 0 if step < 0 else place < size
            exists = inside if exists is None else exists & inside
    return target, exists


def source_slice(step, count):
    return pl.ds(0, count) if step == 0 else pl.ds(count - 1 if step > 0 else 0, 1)


def halo_slice(step, count):
    return pl.ds(1, count) if step == 0 else pl.ds(0 if step > 0 else count + 1, 1)


def exchange_body(sizes, fill, source_ref, padded_ref, send_sems, recv_sems):
    extent = tuple(size - 2 for size in padded_ref.shape[:3])
    barrier = pltpu.get_barrier_semaphore()
    places = {offset: beside(offset, sizes) for offset in AROUND}
    for offset in AROUND:
        target, exists = places[offset]

        def greet(target=target):
            pl.semaphore_signal(barrier, inc=1, device_id=target, device_id_type=MESH)

        when(exists, greet)
    fill()
    copies = {}
    for number, offset in enumerate(AROUND):
        target, exists = places[offset]
        back = tuple(-step for step in offset)
        area = tuple(halo_slice(back[k], extent[k]) for k in range(3))
        if exists is not None:

            def blank(area=area):
                shape = tuple(part.size for part in area) + padded_ref.shape[3:]
                padded_ref[area] = jnp.zeros(shape, jnp.float32)

            pl.when(jnp.logical_not(exists))(blank)
        copies[offset] = pltpu.make_async_remote_copy(
            src_ref=source_ref.at[tuple(source_slice(offset[k], extent[k]) for k in range(3))],
            dst_ref=padded_ref.at[tuple(halo_slice(offset[k], extent[k]) for k in range(3))],
            send_sem=send_sems.at[number],
            recv_sem=recv_sems.at[number],
            device_id=target,
            device_id_type=MESH,
        )
    around = 3
    for axis, size in (("gy", sizes[1]), ("gz", sizes[2])):
        place = lax.axis_index(axis)
        around = around * (1 + jnp.minimum(place, 1) + jnp.minimum(size - 1 - place, 1))
    pl.semaphore_wait(barrier, around - 1)
    for offset in AROUND:
        when(places[offset][1], copies[offset].start)
    for offset in AROUND:
        back = tuple(-step for step in offset)
        when(places[back][1], copies[offset].wait_recv)
    for offset in AROUND:
        when(places[offset][1], copies[offset].wait_send)


def exchange_kernel(sizes, tile_ref, padded_ref, send_sems, recv_sems):
    cx, cy, cz = tile_ref.shape[:3]

    def fill():
        padded_ref[1 : 1 + cx, 1 : 1 + cy, 1 : 1 + cz] = tile_ref[...]

    exchange_body(sizes, fill, tile_ref, padded_ref, send_sems, recv_sems)


def first_kernel(
    sizes, count_hbm, pos_hbm, vel_hbm, force_hbm, seed_hbm, padded_ref, state_ref,
    count_ref, pos_ref, vel_ref, force_ref, seed_ref, load_sems, tile_ref, send_sems, recv_sems,
):
    loads = []
    for number, (source, target) in enumerate(
        (
            (count_hbm, count_ref),
            (pos_hbm, pos_ref),
            (vel_hbm, vel_ref),
            (force_hbm, force_ref),
            (seed_hbm, seed_ref),
        )
    ):
        loads.append(pltpu.make_async_copy(source, target, load_sems.at[number]))
        loads[-1].start()
    cx, cy, cz = tile_ref.shape[:3]
    slot = lax.broadcasted_iota(jnp.int32, (1, LANES), 1)

    def fill():
        for load in loads:
            load.wait()
        for ix in range(cx):
            for iy in range(cy):
                for iz in range(cz):
                    pos, vel, force = [
                        ref[:, ix, iy, iz, :] for ref in (pos_ref, vel_ref, force_ref)
                    ]
                    seed = seed_ref[ix, iy, iz : iz + 1, :].astype(jnp.float32)
                    here = jnp.where(slot < count_ref[ix, iy, iz], 1.0, 0.0)
                    pos = pos + time_step * vel + 0.5 * time_step * time_step * force
                    guessed = vel + predict_weight * time_step * force
                    for ref, top, low, mark in (
                        (tile_ref, pos, friction * guessed, centred(seed, 3)),
                        (state_ref, vel, force, seed),
                    ):
                        ref[ix, iy, iz, 0:3, :] = top
                        ref[ix, iy, iz, 3:6, :] = low
                        ref[ix, iy, iz, 6:7, :] = mark
                        ref[ix, iy, iz, 7:8, :] = here
        padded_ref[1 : 1 + cx, 1 : 1 + cy, 1 : 1 + cz] = tile_ref[...]

    exchange_body(sizes, fill, tile_ref, padded_ref, send_sems, recv_sems)


def mesh_sizes():
    return tuple(lax.axis_size(axis) for axis in ("gx", "gy", "gz"))


def padded_shape(extent):
    return tuple(size + 2 for size in extent) + (ROWS, LANES)


def exchange_sems():
    return [pltpu.SemaphoreType.DMA((len(AROUND),)), pltpu.SemaphoreType.DMA((len(AROUND),))]


def comm_params(number):
    return pltpu.CompilerParams(
        collective_id=number, has_side_effects=True, vmem_limit_bytes=32 * 1024 * 1024
    )


def exchange_call(tile):
    return pl.pallas_call(
        functools.partial(exchange_kernel, mesh_sizes()),
        out_shape=jax.ShapeDtypeStruct(padded_shape(tile.shape[:3]), jnp.float32),
        in_specs=[VMEM_SPEC],
        out_specs=VMEM_SPEC,
        scratch_shapes=exchange_sems(),
        compiler_params=comm_params(1),
        name="exchange",
    )(tile)


def first_call(cell_count, bead_pos, bead_vel, bead_force, pair_seed):
    extent = cell_count.shape
    return pl.pallas_call(
        functools.partial(first_kernel, mesh_sizes()),
        out_shape=(
            jax.ShapeDtypeStruct(padded_shape(extent), jnp.float32),
            jax.ShapeDtypeStruct(extent + (ROWS, LANES), jnp.float32),
        ),
        in_specs=[HBM_SPEC] * 5,
        out_specs=(VMEM_SPEC, VMEM_SPEC),
        scratch_shapes=[
            pltpu.SMEM(extent, jnp.int32),
            pltpu.VMEM(bead_pos.shape, jnp.float32),
            pltpu.VMEM(bead_pos.shape, jnp.float32),
            pltpu.VMEM(bead_pos.shape, jnp.float32),
            pltpu.VMEM(pair_seed.shape, jnp.int32),
            pltpu.SemaphoreType.DMA((5,)),
            pltpu.VMEM(extent + (ROWS, LANES), jnp.float32),
        ]
        + exchange_sems(),
        compiler_params=comm_params(2),
        name="first_exchange",
    )(cell_count, bead_pos, bead_vel, bead_force, pair_seed)


def gather_kernel(
    sizes, state_ref, half_hbm, grid_hbm, map_hbm, whole,
    half_ref, grid_ref, map_ref, load_sems, mine, plane, slots, send_sems, recv_sems,
):
    loads = []
    for number, (source, target) in enumerate(
        ((half_hbm, half_ref), (grid_hbm, grid_ref), (map_hbm, map_ref))
    ):
        loads.append(pltpu.make_async_copy(source, target, load_sems.at[number]))
        loads[-1].start()
    nx, ny, nz = sizes
    cx, cy, cz = state_ref.shape[:3]
    rows, depth = grid_ref.shape[2:]
    span = mine.shape[2]
    count_y = span // depth
    here = (lax.axis_index("gx"), lax.axis_index("gy"), lax.axis_index("gz"))
    barrier = pltpu.get_barrier_semaphore()
    across, along = [], []
    for step_y in range(ny):
        for step_z in range(nz):
            if step_y + step_z > 0:
                place_y = lax.rem(here[1] + step_y, ny)
                across.append((here[0], place_y, lax.rem(here[2] + step_z, nz)))
    for step in range(1, nx):
        along.append((lax.rem(here[0] + step, nx), here[1], here[2]))
    for target in across + along:
        pl.semaphore_signal(barrier, inc=1, device_id=target, device_id_type=MESH)

    for load in loads:
        load.wait()
    lane = lax.broadcasted_iota(jnp.int32, (ROWS, span), 1)
    row_id = lax.broadcasted_iota(jnp.int32, (ROWS, LANES), 0)
    for ix in range(cx):
        placed = jnp.zeros((ROWS, span), jnp.float32)
        for row in range(rows):
            mine[ix] = jnp.zeros((ROWS, span), jnp.float32)
            for k in range(3):
                mine[ix, 4 + k : 5 + k, 0:depth] = grid_ref[k, ix, row : row + 1, :]
            mine[ix, 7:8, 0:depth] = map_ref[ix, row : row + 1, :].astype(jnp.float32)
            at = ((here[1] * nz + here[2]) * rows + row) * depth
            placed = placed + pltpu.roll(mine[ix], at, 1)
        for iy in range(cy):
            for iz in range(cz):
                tile = state_ref[ix, iy, iz]
                values = jnp.where(row_id < 3, tile, jnp.where(row_id == 3, 1.0, 0.0))
                values = jnp.where(tile[7:8, :] > 0.5, values, 0.0)
                half = half_ref[ix, iy, iz : iz + 1, :]
                for side in (0, 1):
                    total = jnp.sum(
                        jnp.where(half == side, values, 0.0), axis=1, keepdims=True
                    )
                    at = (here[1] * cy + iy) * depth + (here[2] * cz + iz) * 2 + side
                    placed = placed + jnp.where(lane == at, total, 0.0)
        mine[ix] = placed

    pl.semaphore_wait(barrier, len(across) + len(along))

    def send_all(targets, source, landings, first):
        copies = []
        for number, target in enumerate(targets):
            copies.append(
                pltpu.make_async_remote_copy(
                    src_ref=source,
                    dst_ref=landings[number],
                    send_sem=send_sems.at[first + number],
                    recv_sem=recv_sems.at[first + number],
                    device_id=target,
                    device_id_type=MESH,
                )
            )
        for copy in copies:
            copy.start()
        return copies

    copies = send_all(across, mine, [slots.at[k] for k in range(len(across))], 0)
    for copy in copies:
        copy.wait_recv()
    total = mine[...]
    for number in range(len(across)):
        total = total + slots[number]
    plane[...] = total
    band = pl.ds(here[0] * cx, cx)
    later = send_all(along, plane, [whole.at[band]] * len(along), len(across))
    whole[band] = total
    for copy in later:
        copy.wait()
    for copy in copies:
        copy.wait_send()


def project_kernel(sizes, extent, rows, depth, whole, grid_out, pressure_out, brick_out, fields):
    nx, ny, nz = sizes
    cx, cy, cz = extent
    span = whole.shape[2]
    count_y = span // depth
    here = (lax.axis_index("gx"), lax.axis_index("gy"), lax.axis_index("gz"))
    parts = [whole[:, k, :] for k in range(8)]
    lanes = lax.broadcasted_iota(jnp.int32, parts[0].shape, 1)
    place_z = lax.rem(lanes, depth)
    place_y = lanes // depth
    count_x = parts[0].shape[0]

    def after(field, axis):
        if axis == 0:
            return pltpu.roll(field, count_x - 1, 0)
        if axis == 1:
            return jnp.where(place_y == count_y - 1, 0.0, pltpu.roll(field, span - depth, 1))
        return jnp.where(place_z == depth - 1, 0.0, pltpu.roll(field, span - 1, 1))

    def prior(field, axis):
        if axis == 0:
            return pltpu.roll(field, 1, 0)
        if axis == 1:
            return jnp.where(place_y == 0, 0.0, pltpu.roll(field, depth, 1))
        return jnp.where(place_z == 0, 0.0, pltpu.roll(field, 1, 1))

    def total_of(field):
        return jnp.sum(jnp.sum(field, axis=0, keepdims=True), axis=1, keepdims=True)

    share = jnp.maximum(parts[3], 1.0)
    coupled = [
        parts[4 + k] + couple_rate * parts[7] * (parts[k] / share - parts[4 + k])
        for k in range(3)
    ]
    divergence = 0.0
    for k in range(3):
        divergence = divergence + after(coupled[k], k) - prior(coupled[k], k)
    residual = -0.5 * divergence
    direction = residual
    pressure = jnp.zeros_like(residual)
    norm_now = total_of(residual * residual)
    for repeat in range(ITERS):
        around = 0.0
        for k in range(3):
            around = around + after(direction, k) + prior(direction, k)
        applied = 6.0 * direction - around
        step_length = norm_now / total_of(direction * applied)
        pressure = pressure + step_length * direction
        residual = residual - step_length * applied
        norm_next = total_of(residual * residual)
        direction = residual + norm_next / norm_now * direction
        norm_now = norm_next
    for k in range(3):
        fields[:, k, :] = coupled[k] - 0.5 * (after(pressure, k) - prior(pressure, k))
    fields[:, 3, :] = pressure
    for ix in range(cx):
        own = fields[here[0] * cx + ix]
        for row in range(rows):
            start = ((here[1] * nz + here[2]) * rows + row) * depth
            band = pltpu.roll(own, lax.rem(span - start, span), 1)
            for k in range(3):
                grid_out[k, ix, row : row + 1, :] = band[k : k + 1, 0:depth]
            pressure_out[ix, row : row + 1, :] = band[3:4, 0:depth]
        for iy in range(cy):
            start = (here[1] * cy + iy) * depth + here[2] * cz * 2
            band = pltpu.roll(own, lax.rem(span - start, span), 1)
            for k in range(3):
                brick_out[k, ix, iy : iy + 1, :] = band[k : k + 1, 0 : cz * 2]


def project_call(state, bead_half, grid_vel, correlation_map):
    sizes = mesh_sizes()
    nx, ny, nz = sizes
    cx, cy, cz = state.shape[:3]
    depth = grid_vel.shape[3]
    span = ny * cy * depth
    shape = (cx, ROWS, span)
    across = max(ny * nz - 1, 1)
    peers = max(ny * nz + nx - 2, 1)
    whole = jax.ShapeDtypeStruct((nx * cx, ROWS, span), jnp.float32)
    gathered = pl.pallas_call(
        functools.partial(gather_kernel, sizes),
        out_shape=whole,
        in_specs=[VMEM_SPEC] + [HBM_SPEC] * 3,
        out_specs=VMEM_SPEC,
        scratch_shapes=[
            pltpu.VMEM(bead_half.shape, jnp.int32),
            pltpu.VMEM(grid_vel.shape, jnp.float32),
            pltpu.VMEM(correlation_map.shape, jnp.int32),
            pltpu.SemaphoreType.DMA((3,)),
            pltpu.VMEM(shape, jnp.float32),
            pltpu.VMEM(shape, jnp.float32),
            pltpu.VMEM((across,) + shape, jnp.float32),
            pltpu.SemaphoreType.DMA((peers,)),
            pltpu.SemaphoreType.DMA((peers,)),
        ],
        compiler_params=comm_params(3),
        name="gather_grid",
    )(state, bead_half, grid_vel, correlation_map)
    return pl.pallas_call(
        functools.partial(project_kernel, sizes, (cx, cy, cz), grid_vel.shape[2], depth),
        out_shape=(
            jax.ShapeDtypeStruct(grid_vel.shape, jnp.float32),
            jax.ShapeDtypeStruct(correlation_map.shape, jnp.float32),
            jax.ShapeDtypeStruct((3, cx, cy, cz * 2), jnp.float32),
        ),
        in_specs=[VMEM_SPEC],
        out_specs=(VMEM_SPEC,) * 3,
        scratch_shapes=[pltpu.VMEM(whole.shape, jnp.float32)],
        compiler_params=pltpu.CompilerParams(vmem_limit_bytes=32 * 1024 * 1024),
        name="project",
    )(gathered)


def per_device(
    bead_pos, bead_vel, bead_force, cell_count, pair_seed, bead_half, grid_vel, correlation_map
):
    padded, state = first_call(cell_count, bead_pos, bead_vel, bead_force, pair_seed)
    for step_number in range(STEPS):
        step_tag = step_number + 3
        if step_number > 0:
            padded = exchange_call(tile)
        tile, *selection = force_call(step_tag, 0, padded, state)
        padded = exchange_call(tile)
        if step_number < STEPS - 1:
            tile, state = force_call(step_tag, 1, padded, state, *selection)
    state, position, velocity = force_call(step_tag, 2, padded, state, *selection)
    return (position, velocity, *project_call(state, bead_half, grid_vel, correlation_map))


def solution(mesh):
    placed = (
        P(None, "gx", "gy", "gz", None),
        P(None, "gx", "gy", "gz", None),
        P(None, "gx", "gy", "gz", None),
        P("gx", "gy", "gz"),
        P("gx", "gy", "gz", None),
        P("gx", "gy", "gz", None),
        P(None, "gx", ("gy", "gz"), None),
        P("gx", ("gy", "gz"), None),
    )
    return jax.shard_map(
        per_device,
        mesh=mesh,
        in_specs=placed,
        out_specs=(
            P(None, "gx", "gy", "gz", None),
            P(None, "gx", "gy", "gz", None),
            P(None, "gx", ("gy", "gz"), None),
            P("gx", ("gy", "gz"), None),
            P(None, "gx", "gy", "gz"),
        ),
        check_vma=False,
    )
```

```python
import functools
import math

import jax
import jax.numpy as jnp
from jax import lax
from jax.experimental import pallas as pl
from jax.experimental.pallas import tpu as pltpu
from jax.sharding import PartitionSpec as P

STEPS = 2
ITERS = 4

cell_edge = 3.0
conserve = 25.0
friction = 4.5
noise_scale = 3.0 * math.sqrt(12.0) / math.sqrt(0.04)
time_step = 0.04
predict_weight = 0.65
couple_rate = 0.5
hash_prime = 4093

LANES = 128
ROWS = 8
BLOCK = 32
FAR = 1.0e15
NEAR = [(ox, oy, oz) for ox in (-1, 0, 1) for oy in (-1, 0, 1) for oz in (-1, 0, 1)]


VMEM_SPEC = pl.BlockSpec(memory_space=pltpu.VMEM)
HBM_SPEC = pl.BlockSpec(memory_space=pltpu.HBM)


def pair_terms(own, chunk, step_tag):
    deltas = [own[k] - chunk[k] for k in range(3)]
    square = deltas[0] * deltas[0] + deltas[1] * deltas[1] + deltas[2] * deltas[2]
    weight = jnp.maximum(1.0 - square, 0.0)
    closing = deltas[0] * (own[3] - chunk[3])
    closing = closing + deltas[1] * (own[4] - chunk[4])
    closing = closing + deltas[2] * (own[5] - chunk[5])
    turns = own[6] * chunk[6] + (0.5 - step_tag * step_tag) / hash_prime
    part = turns - jnp.floor(turns)
    steady = part * noise_scale + (conserve - (0.5 + 0.5 / hash_prime) * noise_scale)
    strength = weight * (steady - weight * closing)
    return [strength * deltas[k] for k in range(3)]


def centred(seed, step_tag):
    moved = seed + float(step_tag)
    return jnp.where(moved > 2046.0, moved - float(hash_prime), moved)


def select_beads(padded_ref, rows_x, masks, index_ref, base_ref):
    px, py, pz = padded_ref.shape[:3]
    cx, cy, cz = px - 2, py - 2, pz - 2
    cells = cx * cy * cz
    for ix in range(px):
        for iz in range(pz):
            present = padded_ref[ix, :, iz, 7, :] > 0.5
            for k in range(3):
                rows_x[k, ix, iz, 0:py, :] = jnp.where(present, padded_ref[ix, :, iz, k, :], FAR)

    for ix in range(cx):
        for iz in range(cz):
            row = (ix * cz + iz) * cy
            low, high = [], []
            for k in range(3):
                mine = rows_x[k, 1 + ix, 1 + iz, 1 : 1 + cy, :]
                there = mine < 0.1 * FAR
                if k == 0:
                    held = jnp.sum(jnp.where(there, 1.0, 0.0), axis=1, keepdims=True)
                least = jnp.min(jnp.where(there, mine, FAR), axis=1, keepdims=True)
                most = jnp.max(jnp.where(there, mine, -FAR), axis=1, keepdims=True)
                low.append(least - 1.001 - 1e-6 * jnp.abs(least))
                high.append(most + 1.001 + 1e-6 * jnp.abs(most))
            base_ref[row : row + cy, :] = jnp.broadcast_to(held, (cy, LANES)).astype(jnp.int32)
            for n, offset in enumerate(NEAR):
                keep = None
                for k in range(3):
                    near = rows_x[
                        k, 1 + ix + offset[0], 1 + iz + offset[2], 1 + offset[1] : 1 + offset[1] + cy, :
                    ]
                    shift = cell_edge * offset[k]
                    inside = (near >= low[k] - shift) & (near <= high[k] - shift)
                    keep = inside if keep is None else keep & inside
                masks[n * cells + row : n * cells + row + cy, :] = jnp.where(keep, 1.0, 0.0)

    mask = masks[...]
    before = lax.broadcasted_iota(jnp.int32, (LANES, LANES), 0)
    after = lax.broadcasted_iota(jnp.int32, (LANES, LANES), 1)
    upper = jnp.where(before < after, 1.0, 0.0).astype(jnp.bfloat16)
    ones = jnp.ones((LANES, LANES), jnp.bfloat16)
    mask16 = mask.astype(jnp.bfloat16)
    rank = jnp.dot(mask16, upper, preferred_element_type=jnp.float32).astype(jnp.int32)
    count = jnp.dot(mask16, ones, preferred_element_type=jnp.float32).astype(jnp.int32)
    spot = lax.broadcasted_iota(jnp.int32, mask.shape, 1)
    entry = jnp.where(mask > 0.5, (spot - rank) * LANES + spot, spot)
    for bit in range(7):
        width = 1 << bit
        flag = LANES << bit
        moved = pltpu.roll(entry, LANES - width, 1)
        stay = jnp.where((entry & flag) != 0, entry & (LANES - 1), entry)
        entry = jnp.where((moved & flag) != 0, moved, stay)
    entry = entry & (LANES - 1)
    bases = []
    running = jnp.zeros((cells, LANES), jnp.int32)
    table = base_ref[...]
    spot_cells = lax.broadcasted_iota(jnp.int32, (cells, LANES), 1)
    for n in range(len(NEAR)):
        bases.append(running)
        table = jnp.where(spot_cells == n, running, table)
        running = running + count[n * cells : (n + 1) * cells, :]
    base_ref[...] = jnp.where(spot_cells == len(NEAR), running, table)
    base_all = jnp.concatenate(bases, axis=0)
    for bit in range(7):
        width = 1 << bit
        entry = jnp.where((base_all & width) != 0, pltpu.roll(entry, width, 1), entry)
    index_ref[...] = entry


def force_kernel(step_tag, phase, padded_ref, state_ref, *refs):
    if phase == 0:
        tile_out, index_ref, base_ref, *scratch = refs
    elif phase == 1:
        index_ref, base_ref, tile_out, state_out, *scratch = refs
    else:
        index_ref, base_ref, state_out, pos_out, vel_out, *scratch = refs
    rows_x, masks, shifts, base_smem, list_ref, own_wide, force_wide, spreader, copy_sem = scratch
    px, py, pz = padded_ref.shape[:3]
    cx, cy, cz = px - 2, py - 2, pz - 2
    cells = cx * cy * cz
    if phase == 0:
        select_beads(padded_ref, rows_x, masks, index_ref, base_ref)
    to_smem = pltpu.make_async_copy(base_ref, base_smem, copy_sem)
    to_smem.start()
    lane = lax.broadcasted_iota(jnp.int32, (ROWS, LANES), 1)
    row_id = lax.broadcasted_iota(jnp.int32, (ROWS, LANES), 0)
    for n, offset in enumerate(NEAR):
        shift = jnp.zeros((ROWS, LANES), jnp.float32)
        for k in range(3):
            shift = jnp.where(row_id == k, cell_edge * offset[k], shift)
        shifts[n] = shift
    force_wide[...] = jnp.zeros(force_wide.shape, jnp.float32)
    from_row = lax.broadcasted_iota(jnp.int32, spreader.shape, 0) & (ROWS - 1)
    to_part = lax.broadcasted_iota(jnp.int32, spreader.shape, 1) >> 7
    spreader[...] = jnp.where(from_row == to_part, 1.0, 0.0).astype(jnp.bfloat16)
    zero = jnp.zeros((BLOCK, LANES), jnp.float32)
    to_smem.wait()

    def place(cell):
        return cell // (cy * cz), cell % cy, (cell // cy) % cz

    def prepare(cell, slot):
        ix, iy, iz = place(cell)
        current = jnp.zeros((ROWS, LANES), jnp.float32)
        for n, offset in enumerate(NEAR):
            tile = padded_ref[ix + 1 + offset[0], iy + 1 + offset[1], iz + 1 + offset[2]]
            index = jnp.broadcast_to(index_ref[pl.ds(n * cells + cell, 1), :], (ROWS, LANES))
            found = jnp.take_along_axis(tile, index, axis=1) + shifts[n]
            base = base_smem[cell, n]
            following = base_smem[cell, n + 1]
            merged = jnp.where(lane >= (base & (LANES - 1)), found, current)
            list_ref[slot, base >> 7] = merged
            crossed = (following >> 7) > (base >> 7)
            current = jnp.where(crossed, found, merged)
        total = base_smem[cell, len(NEAR)]
        list_ref[slot, total >> 7] = jnp.where(
            (row_id == 0) & (lane >= (total & (LANES - 1))), -FAR, current
        )
        own_tile = padded_ref[ix + 1, iy + 1, iz + 1]
        parts, left = [], own_tile
        for level in range(3):
            parts.append(left.astype(jnp.bfloat16).astype(jnp.float32))
            left = left - parts[-1]
        parts.append(jnp.zeros_like(own_tile))
        own_cols = jnp.concatenate(parts, axis=0).T.astype(jnp.bfloat16)
        spread = jnp.dot(own_cols, spreader[...], preferred_element_type=jnp.float32)
        for k in range(7):
            own_wide[slot, k] = spread[:, k * LANES : (k + 1) * LANES]

    prepare(0, 0)

    def one_cell(cell, carry):
        ix, iy, iz = place(cell)
        slot = cell & 1
        chunks = (base_smem[cell, len(NEAR)] + LANES - 1) >> 7
        blocks = (base_smem[cell, len(NEAR) + 1] + BLOCK - 1) // BLOCK

        def one_block(block, carry):
            at = pl.multiple_of(block * BLOCK, BLOCK)
            own = [own_wide[slot, k, pl.ds(at, BLOCK), :] for k in range(7)]
            own[6] = own[6] * (1.0 / hash_prime)

            def one_chunk(index, sums):
                chunk = [list_ref[slot, index, k : k + 1, :] for k in range(7)]
                terms = pair_terms(own, chunk, step_tag)
                return tuple(sums[k] + terms[k] for k in range(3))

            sums = lax.fori_loop(0, chunks, one_chunk, (zero, zero, zero))
            for k in range(3):
                force_wide[k, pl.ds(at, BLOCK), :] = sums[k]
            return carry

        lax.fori_loop(0, blocks, one_block, 0)
        prepare(jnp.minimum(cell + 1, cells - 1), 1 - slot)
        own_tile = padded_ref[ix + 1, iy + 1, iz + 1]
        wide = force_wide[...].reshape(3 * LANES, LANES)
        coarse = wide.astype(jnp.bfloat16)
        fine = (wide - coarse.astype(jnp.float32)).astype(jnp.bfloat16)
        summed = lax.dot_general(
            jnp.ones((ROWS, 2 * LANES), jnp.bfloat16),
            jnp.concatenate([coarse, fine], axis=1),
            (((1,), (1,)), ((), ())),
            preferred_element_type=jnp.float32,
        )
        state = state_ref[ix, iy, iz]
        new_vel, force = [], []
        for k in range(3):
            row = summed[0:1, k * LANES : (k + 1) * LANES]
            row = jnp.where(own_tile[7:8, :] > 0.5, row, 0.0)
            force.append(row)
            new_vel.append(
                state[k : k + 1, :] + 0.5 * time_step * (state[3 + k : 4 + k, :] + row)
            )
        if phase == 0:
            for k in range(3):
                tile_out[ix, iy, iz, k : k + 1, :] = own_tile[k : k + 1, :]
                tile_out[ix, iy, iz, 3 + k : 4 + k, :] = friction * new_vel[k]
            tile_out[ix, iy, iz, 6:8, :] = own_tile[6:8, :]
            return carry
        for k in range(3):
            state_out[ix, iy, iz, k : k + 1, :] = new_vel[k]
            state_out[ix, iy, iz, 3 + k : 4 + k, :] = force[k]
        state_out[ix, iy, iz, 6:8, :] = state[6:8, :]
        for k in range(3):
            position = own_tile[k : k + 1, :]
            if phase == 2:
                pos_out[k, ix, iy, pl.ds(iz, 1), :] = position
                vel_out[k, ix, iy, pl.ds(iz, 1), :] = new_vel[k]
                continue
            position = position + time_step * new_vel[k]
            position = position + 0.5 * time_step * time_step * force[k]
            tile_out[ix, iy, iz, k : k + 1, :] = position
            guessed = new_vel[k] + predict_weight * time_step * force[k]
            tile_out[ix, iy, iz, 3 + k : 4 + k, :] = friction * guessed
        if phase == 1:
            tile_out[ix, iy, iz, 6:7, :] = centred(state[6:7, :], step_tag + 1)
            tile_out[ix, iy, iz, 7:8, :] = state[7:8, :]
        return carry

    lax.fori_loop(0, cells, one_cell, 0)


def force_call(step_tag, phase, padded, state, *selection):
    px, py, pz = padded.shape[:3]
    cx, cy, cz = state.shape[:3]
    cells = cx * cy * cz
    near = len(NEAR)
    tall = -(-py // 8) * 8
    brick = jax.ShapeDtypeStruct(state.shape, jnp.float32)
    beads = jax.ShapeDtypeStruct((3, cx, cy, cz, LANES), jnp.float32)
    if phase == 0:
        index = jax.ShapeDtypeStruct((near * cells, LANES), jnp.int32)
        outs = (brick, index, jax.ShapeDtypeStruct((cells, LANES), jnp.int32))
    else:
        outs = (brick, brick) if phase == 1 else (brick, beads, beads)
    return pl.pallas_call(
        functools.partial(force_kernel, step_tag, phase),
        out_shape=outs,
        in_specs=[VMEM_SPEC] * (2 + len(selection)),
        out_specs=(VMEM_SPEC,) * len(outs),
        scratch_shapes=[
            pltpu.VMEM((3, px, pz, tall, LANES), jnp.float32),
            pltpu.VMEM((near * cells, LANES), jnp.float32),
            pltpu.VMEM((near, ROWS, LANES), jnp.float32),
            pltpu.SMEM((cells, LANES), jnp.int32),
            pltpu.VMEM((2, near + 1, ROWS, LANES), jnp.float32),
            pltpu.VMEM((2, 7, LANES, LANES), jnp.float32),
            pltpu.VMEM((3, LANES, LANES), jnp.float32),
            pltpu.VMEM((4 * ROWS, 7 * LANES), jnp.bfloat16),
            pltpu.SemaphoreType.DMA,
        ],
        compiler_params=pltpu.CompilerParams(vmem_limit_bytes=32 * 1024 * 1024),
        name="pair_forces",
    )(padded, state, *selection)


MESH = pl.DeviceIdType.MESH
AROUND = sorted(
    (offset for offset in NEAR if offset != (0, 0, 0)),
    key=lambda offset: sum(abs(step) for step in offset),
)


def when(condition, body):
    if condition is None:
        body()
    else:
        pl.when(condition)(body)


def beside(offset, sizes):
    nx, ny, nz = sizes
    target = (
        lax.rem(lax.axis_index("gx") + (offset[0] + nx), nx),
        lax.axis_index("gy") + offset[1],
        lax.axis_index("gz") + offset[2],
    )
    exists = None
    for step, place, size in ((offset[1], target[1], ny), (offset[2], target[2], nz)):
        if step != 0:
            inside = place >= 0 if step < 0 else place < size
            exists = inside if exists is None else exists & inside
    return target, exists


def source_slice(step, count):
    return pl.ds(0, count) if step == 0 else pl.ds(count - 1 if step > 0 else 0, 1)


def halo_slice(step, count):
    return pl.ds(1, count) if step == 0 else pl.ds(0 if step > 0 else count + 1, 1)


def exchange_body(sizes, fill, source_ref, padded_ref, send_sems, recv_sems):
    extent = tuple(size - 2 for size in padded_ref.shape[:3])
    barrier = pltpu.get_barrier_semaphore()
    places = {offset: beside(offset, sizes) for offset in AROUND}
    for offset in AROUND:
        target, exists = places[offset]

        def greet(target=target):
            pl.semaphore_signal(barrier, inc=1, device_id=target, device_id_type=MESH)

        when(exists, greet)
    fill()
    copies = {}
    for number, offset in enumerate(AROUND):
        target, exists = places[offset]
        back = tuple(-step for step in offset)
        area = tuple(halo_slice(back[k], extent[k]) for k in range(3))
        if exists is not None:

            def blank(area=area):
                shape = tuple(part.size for part in area) + padded_ref.shape[3:]
                padded_ref[area] = jnp.zeros(shape, jnp.float32)

            pl.when(jnp.logical_not(exists))(blank)
        copies[offset] = pltpu.make_async_remote_copy(
            src_ref=source_ref.at[tuple(source_slice(offset[k], extent[k]) for k in range(3))],
            dst_ref=padded_ref.at[tuple(halo_slice(offset[k], extent[k]) for k in range(3))],
            send_sem=send_sems.at[number],
            recv_sem=recv_sems.at[number],
            device_id=target,
            device_id_type=MESH,
        )
    around = 3
    for axis, size in (("gy", sizes[1]), ("gz", sizes[2])):
        place = lax.axis_index(axis)
        around = around * (1 + jnp.minimum(place, 1) + jnp.minimum(size - 1 - place, 1))
    pl.semaphore_wait(barrier, around - 1)
    for offset in AROUND:
        when(places[offset][1], copies[offset].start)
    for offset in AROUND:
        back = tuple(-step for step in offset)
        when(places[back][1], copies[offset].wait_recv)
    for offset in AROUND:
        when(places[offset][1], copies[offset].wait_send)


def exchange_kernel(sizes, tile_ref, padded_ref, send_sems, recv_sems):
    cx, cy, cz = tile_ref.shape[:3]

    def fill():
        padded_ref[1 : 1 + cx, 1 : 1 + cy, 1 : 1 + cz] = tile_ref[...]

    exchange_body(sizes, fill, tile_ref, padded_ref, send_sems, recv_sems)


def first_kernel(
    sizes, count_hbm, pos_hbm, vel_hbm, force_hbm, seed_hbm, padded_ref, state_ref,
    count_ref, pos_ref, vel_ref, force_ref, seed_ref, load_sems, tile_ref, send_sems, recv_sems,
):
    loads = []
    for number, (source, target) in enumerate(
        (
            (count_hbm, count_ref),
            (pos_hbm, pos_ref),
            (vel_hbm, vel_ref),
            (force_hbm, force_ref),
            (seed_hbm, seed_ref),
        )
    ):
        loads.append(pltpu.make_async_copy(source, target, load_sems.at[number]))
        loads[-1].start()
    cx, cy, cz = tile_ref.shape[:3]
    slot = lax.broadcasted_iota(jnp.int32, (1, LANES), 1)

    def fill():
        for load in loads:
            load.wait()
        for ix in range(cx):
            for iy in range(cy):
                for iz in range(cz):
                    pos, vel, force = [
                        ref[:, ix, iy, iz, :] for ref in (pos_ref, vel_ref, force_ref)
                    ]
                    seed = seed_ref[ix, iy, iz : iz + 1, :].astype(jnp.float32)
                    here = jnp.where(slot < count_ref[ix, iz, iy], 1.0, 0.0)
                    pos = pos + time_step * vel + 0.5 * time_step * time_step * force
                    guessed = vel + predict_weight * time_step * force
                    for ref, top, low, mark in (
                        (tile_ref, pos, friction * guessed, centred(seed, 3)),
                        (state_ref, vel, force, seed),
                    ):
                        ref[ix, iy, iz, 0:3, :] = top
                        ref[ix, iy, iz, 3:6, :] = low
                        ref[ix, iy, iz, 6:7, :] = mark
                        ref[ix, iy, iz, 7:8, :] = here
        padded_ref[1 : 1 + cx, 1 : 1 + cy, 1 : 1 + cz] = tile_ref[...]

    exchange_body(sizes, fill, tile_ref, padded_ref, send_sems, recv_sems)


def mesh_sizes():
    return tuple(lax.axis_size(axis) for axis in ("gx", "gy", "gz"))


def padded_shape(extent):
    return tuple(size + 2 for size in extent) + (ROWS, LANES)


def exchange_sems():
    return [pltpu.SemaphoreType.DMA((len(AROUND),)), pltpu.SemaphoreType.DMA((len(AROUND),))]


def comm_params(number):
    return pltpu.CompilerParams(
        collective_id=number, has_side_effects=True, vmem_limit_bytes=32 * 1024 * 1024
    )


def exchange_call(tile):
    return pl.pallas_call(
        functools.partial(exchange_kernel, mesh_sizes()),
        out_shape=jax.ShapeDtypeStruct(padded_shape(tile.shape[:3]), jnp.float32),
        in_specs=[VMEM_SPEC],
        out_specs=VMEM_SPEC,
        scratch_shapes=exchange_sems(),
        compiler_params=comm_params(1),
        name="exchange",
    )(tile)


def first_call(cell_count, bead_pos, bead_vel, bead_force, pair_seed):
    extent = cell_count.shape
    return pl.pallas_call(
        functools.partial(first_kernel, mesh_sizes()),
        out_shape=(
            jax.ShapeDtypeStruct(padded_shape(extent), jnp.float32),
            jax.ShapeDtypeStruct(extent + (ROWS, LANES), jnp.float32),
        ),
        in_specs=[HBM_SPEC] * 5,
        out_specs=(VMEM_SPEC, VMEM_SPEC),
        scratch_shapes=[
            pltpu.SMEM((extent[0], extent[2], extent[1]), jnp.int32),
            pltpu.VMEM(bead_pos.shape, jnp.float32),
            pltpu.VMEM(bead_pos.shape, jnp.float32),
            pltpu.VMEM(bead_pos.shape, jnp.float32),
            pltpu.VMEM(pair_seed.shape, jnp.int32),
            pltpu.SemaphoreType.DMA((5,)),
            pltpu.VMEM(extent + (ROWS, LANES), jnp.float32),
        ]
        + exchange_sems(),
        compiler_params=comm_params(2),
        name="first_exchange",
    )(jnp.swapaxes(cell_count, 1, 2), bead_pos, bead_vel, bead_force, pair_seed)


def gather_kernel(
    sizes, state_ref, half_hbm, grid_hbm, map_hbm, whole,
    half_ref, grid_ref, map_ref, load_sems, mine, plane, slots, send_sems, recv_sems,
):
    loads = []
    for number, (source, target) in enumerate(
        ((half_hbm, half_ref), (grid_hbm, grid_ref), (map_hbm, map_ref))
    ):
        loads.append(pltpu.make_async_copy(source, target, load_sems.at[number]))
        loads[-1].start()
    nx, ny, nz = sizes
    cx, cy, cz = state_ref.shape[:3]
    rows, depth = grid_ref.shape[2:]
    span = mine.shape[2]
    count_y = span // depth
    here = (lax.axis_index("gx"), lax.axis_index("gy"), lax.axis_index("gz"))
    barrier = pltpu.get_barrier_semaphore()
    across, along = [], []
    for step_y in range(ny):
        for step_z in range(nz):
            if step_y + step_z > 0:
                place_y = lax.rem(here[1] + step_y, ny)
                across.append((here[0], place_y, lax.rem(here[2] + step_z, nz)))
    for step in range(1, nx):
        along.append((lax.rem(here[0] + step, nx), here[1], here[2]))
    for target in across + along:
        pl.semaphore_signal(barrier, inc=1, device_id=target, device_id_type=MESH)

    for load in loads:
        load.wait()
    lane = lax.broadcasted_iota(jnp.int32, (ROWS, span), 1)
    row_id = lax.broadcasted_iota(jnp.int32, (ROWS, LANES), 0)
    for ix in range(cx):
        placed = jnp.zeros((ROWS, span), jnp.float32)
        for row in range(rows):
            mine[ix] = jnp.zeros((ROWS, span), jnp.float32)
            for k in range(3):
                mine[ix, 4 + k : 5 + k, 0:depth] = grid_ref[k, ix, row : row + 1, :]
            mine[ix, 7:8, 0:depth] = map_ref[ix, row : row + 1, :].astype(jnp.float32)
            at = ((here[1] * nz + here[2]) * rows + row) * depth
            placed = placed + pltpu.roll(mine[ix], at, 1)
        for iy in range(cy):
            for iz in range(cz):
                tile = state_ref[ix, iy, iz]
                values = jnp.where(row_id < 3, tile, jnp.where(row_id == 3, 1.0, 0.0))
                values = jnp.where(tile[7:8, :] > 0.5, values, 0.0)
                half = half_ref[ix, iy, iz : iz + 1, :]
                for side in (0, 1):
                    total = jnp.sum(
                        jnp.where(half == side, values, 0.0), axis=1, keepdims=True
                    )
                    at = (here[1] * cy + iy) * depth + (here[2] * cz + iz) * 2 + side
                    placed = placed + jnp.where(lane == at, total, 0.0)
        mine[ix] = placed

    pl.semaphore_wait(barrier, len(across) + len(along))

    def send_all(targets, source, landings, first):
        copies = []
        for number, target in enumerate(targets):
            copies.append(
                pltpu.make_async_remote_copy(
                    src_ref=source,
                    dst_ref=landings[number],
                    send_sem=send_sems.at[first + number],
                    recv_sem=recv_sems.at[first + number],
                    device_id=target,
                    device_id_type=MESH,
                )
            )
        for copy in copies:
            copy.start()
        return copies

    copies = send_all(across, mine, [slots.at[k] for k in range(len(across))], 0)
    for copy in copies:
        copy.wait_recv()
    total = mine[...]
    for number in range(len(across)):
        total = total + slots[number]
    plane[...] = total
    band = pl.ds(here[0] * cx, cx)
    later = send_all(along, plane, [whole.at[band]] * len(along), len(across))
    whole[band] = total
    for copy in later:
        copy.wait()
    for copy in copies:
        copy.wait_send()


def project_kernel(sizes, extent, rows, depth, whole, grid_out, pressure_out, brick_out, fields):
    nx, ny, nz = sizes
    cx, cy, cz = extent
    span = whole.shape[2]
    count_y = span // depth
    here = (lax.axis_index("gx"), lax.axis_index("gy"), lax.axis_index("gz"))
    parts = [whole[:, k, :] for k in range(8)]
    lanes = lax.broadcasted_iota(jnp.int32, parts[0].shape, 1)
    place_z = lax.rem(lanes, depth)
    place_y = lanes // depth
    count_x = parts[0].shape[0]

    def after(field, axis):
        if axis == 0:
            return pltpu.roll(field, count_x - 1, 0)
        if axis == 1:
            return jnp.where(place_y == count_y - 1, 0.0, pltpu.roll(field, span - depth, 1))
        return jnp.where(place_z == depth - 1, 0.0, pltpu.roll(field, span - 1, 1))

    def prior(field, axis):
        if axis == 0:
            return pltpu.roll(field, 1, 0)
        if axis == 1:
            return jnp.where(place_y == 0, 0.0, pltpu.roll(field, depth, 1))
        return jnp.where(place_z == 0, 0.0, pltpu.roll(field, 1, 1))

    def total_of(field):
        return jnp.sum(jnp.sum(field, axis=0, keepdims=True), axis=1, keepdims=True)

    share = jnp.maximum(parts[3], 1.0)
    coupled = [
        parts[4 + k] + couple_rate * parts[7] * (parts[k] / share - parts[4 + k])
        for k in range(3)
    ]
    divergence = 0.0
    for k in range(3):
        divergence = divergence + after(coupled[k], k) - prior(coupled[k], k)
    residual = -0.5 * divergence
    direction = residual
    pressure = jnp.zeros_like(residual)
    norm_now = total_of(residual * residual)
    for repeat in range(ITERS):
        around = 0.0
        for k in range(3):
            around = around + after(direction, k) + prior(direction, k)
        applied = 6.0 * direction - around
        step_length = norm_now / total_of(direction * applied)
        pressure = pressure + step_length * direction
        residual = residual - step_length * applied
        norm_next = total_of(residual * residual)
        direction = residual + norm_next / norm_now * direction
        norm_now = norm_next
    for k in range(3):
        fields[:, k, :] = coupled[k] - 0.5 * (after(pressure, k) - prior(pressure, k))
    fields[:, 3, :] = pressure
    for ix in range(cx):
        own = fields[here[0] * cx + ix]
        for row in range(rows):
            start = ((here[1] * nz + here[2]) * rows + row) * depth
            band = pltpu.roll(own, lax.rem(span - start, span), 1)
            for k in range(3):
                grid_out[k, ix, row : row + 1, :] = band[k : k + 1, 0:depth]
            pressure_out[ix, row : row + 1, :] = band[3:4, 0:depth]
        for iy in range(cy):
            start = (here[1] * cy + iy) * depth + here[2] * cz * 2
            band = pltpu.roll(own, lax.rem(span - start, span), 1)
            for k in range(3):
                brick_out[k, ix, iy : iy + 1, :] = band[k : k + 1, 0 : cz * 2]


def project_call(state, bead_half, grid_vel, correlation_map):
    sizes = mesh_sizes()
    nx, ny, nz = sizes
    cx, cy, cz = state.shape[:3]
    depth = grid_vel.shape[3]
    span = ny * cy * depth
    shape = (cx, ROWS, span)
    across = max(ny * nz - 1, 1)
    peers = max(ny * nz + nx - 2, 1)
    whole = jax.ShapeDtypeStruct((nx * cx, ROWS, span), jnp.float32)
    gathered = pl.pallas_call(
        functools.partial(gather_kernel, sizes),
        out_shape=whole,
        in_specs=[VMEM_SPEC] + [HBM_SPEC] * 3,
        out_specs=VMEM_SPEC,
        scratch_shapes=[
            pltpu.VMEM(bead_half.shape, jnp.int32),
            pltpu.VMEM(grid_vel.shape, jnp.float32),
            pltpu.VMEM(correlation_map.shape, jnp.int32),
            pltpu.SemaphoreType.DMA((3,)),
            pltpu.VMEM(shape, jnp.float32),
            pltpu.VMEM(shape, jnp.float32),
            pltpu.VMEM((across,) + shape, jnp.float32),
            pltpu.SemaphoreType.DMA((peers,)),
            pltpu.SemaphoreType.DMA((peers,)),
        ],
        compiler_params=comm_params(3),
        name="gather_grid",
    )(state, bead_half, grid_vel, correlation_map)
    return pl.pallas_call(
        functools.partial(project_kernel, sizes, (cx, cy, cz), grid_vel.shape[2], depth),
        out_shape=(
            jax.ShapeDtypeStruct(grid_vel.shape, jnp.float32),
            jax.ShapeDtypeStruct(correlation_map.shape, jnp.float32),
            jax.ShapeDtypeStruct((3, cx, cy, cz * 2), jnp.float32),
        ),
        in_specs=[VMEM_SPEC],
        out_specs=(VMEM_SPEC,) * 3,
        scratch_shapes=[pltpu.VMEM(whole.shape, jnp.float32)],
        compiler_params=pltpu.CompilerParams(vmem_limit_bytes=32 * 1024 * 1024),
        name="project",
    )(gathered)


def per_device(
    bead_pos, bead_vel, bead_force, cell_count, pair_seed, bead_half, grid_vel, correlation_map
):
    padded, state = first_call(cell_count, bead_pos, bead_vel, bead_force, pair_seed)
    for step_number in range(STEPS):
        step_tag = step_number + 3
        if step_number > 0:
            padded = exchange_call(tile)
        tile, *selection = force_call(step_tag, 0, padded, state)
        padded = exchange_call(tile)
        if step_number < STEPS - 1:
            tile, state = force_call(step_tag, 1, padded, state, *selection)
    state, position, velocity = force_call(step_tag, 2, padded, state, *selection)
    return (position, velocity, *project_call(state, bead_half, grid_vel, correlation_map))


def solution(mesh):
    placed = (
        P(None, "gx", "gy", "gz", None),
        P(None, "gx", "gy", "gz", None),
        P(None, "gx", "gy", "gz", None),
        P("gx", "gy", "gz"),
        P("gx", "gy", "gz", None),
        P("gx", "gy", "gz", None),
        P(None, "gx", ("gy", "gz"), None),
        P("gx", ("gy", "gz"), None),
    )
    return jax.shard_map(
        per_device,
        mesh=mesh,
        in_specs=placed,
        out_specs=(
            P(None, "gx", "gy", "gz", None),
            P(None, "gx", "gy", "gz", None),
            P(None, "gx", ("gy", "gz"), None),
            P("gx", ("gy", "gz"), None),
            P(None, "gx", "gy", "gz"),
        ),
        check_vma=False,
    )
```

```python
import functools
import math

import jax
import jax.numpy as jnp
from jax import lax
from jax.experimental import pallas as pl
from jax.experimental.pallas import tpu as pltpu
from jax.sharding import PartitionSpec as P

STEPS = 2
ITERS = 4

cell_edge = 3.0
conserve = 25.0
friction = 4.5
noise_scale = 3.0 * math.sqrt(12.0) / math.sqrt(0.04)
time_step = 0.04
predict_weight = 0.65
couple_rate = 0.5
hash_prime = 4093

LANES = 128
ROWS = 8
BLOCK = 32
FAR = 1.0e15
NEAR = [(ox, oy, oz) for ox in (-1, 0, 1) for oy in (-1, 0, 1) for oz in (-1, 0, 1)]


VMEM_SPEC = pl.BlockSpec(memory_space=pltpu.VMEM)
HBM_SPEC = pl.BlockSpec(memory_space=pltpu.HBM)


def pair_terms(own, chunk, step_tag):
    deltas = [own[k] - chunk[k] for k in range(3)]
    square = deltas[0] * deltas[0] + deltas[1] * deltas[1] + deltas[2] * deltas[2]
    weight = jnp.maximum(1.0 - square, 0.0)
    closing = deltas[0] * (own[3] - chunk[3])
    closing = closing + deltas[1] * (own[4] - chunk[4])
    closing = closing + deltas[2] * (own[5] - chunk[5])
    turns = own[6] * chunk[6] + (0.5 - step_tag * step_tag) / hash_prime
    part = turns - jnp.floor(turns)
    steady = part * noise_scale + (conserve - (0.5 + 0.5 / hash_prime) * noise_scale)
    strength = weight * (steady - weight * closing)
    return [strength * deltas[k] for k in range(3)]


def centred(seed, step_tag):
    moved = seed + float(step_tag)
    return jnp.where(moved > 2046.0, moved - float(hash_prime), moved)


def select_beads(padded_ref, rows_x, masks, index_ref, base_ref):
    px, py, pz = padded_ref.shape[:3]
    cx, cy, cz = px - 2, py - 2, pz - 2
    cells = cx * cy * cz
    for ix in range(px):
        for iz in range(pz):
            present = padded_ref[ix, :, iz, 7, :] > 0.5
            for k in range(3):
                rows_x[k, ix, iz, 0:py, :] = jnp.where(present, padded_ref[ix, :, iz, k, :], FAR)

    for ix in range(cx):
        for iz in range(cz):
            row = (ix * cz + iz) * cy
            low, high = [], []
            for k in range(3):
                mine = rows_x[k, 1 + ix, 1 + iz, 1 : 1 + cy, :]
                there = mine < 0.1 * FAR
                if k == 0:
                    held = jnp.sum(jnp.where(there, 1.0, 0.0), axis=1, keepdims=True)
                least = jnp.min(jnp.where(there, mine, FAR), axis=1, keepdims=True)
                most = jnp.max(jnp.where(there, mine, -FAR), axis=1, keepdims=True)
                low.append(least - 1.001 - 1e-6 * jnp.abs(least))
                high.append(most + 1.001 + 1e-6 * jnp.abs(most))
            base_ref[row : row + cy, :] = jnp.broadcast_to(held, (cy, LANES)).astype(jnp.int32)
            for n, offset in enumerate(NEAR):
                keep = None
                for k in range(3):
                    near = rows_x[
                        k, 1 + ix + offset[0], 1 + iz + offset[2], 1 + offset[1] : 1 + offset[1] + cy, :
                    ]
                    shift = cell_edge * offset[k]
                    inside = (near >= low[k] - shift) & (near <= high[k] - shift)
                    keep = inside if keep is None else keep & inside
                masks[n * cells + row : n * cells + row + cy, :] = jnp.where(keep, 1.0, 0.0)

    mask = masks[...]
    before = lax.broadcasted_iota(jnp.int32, (LANES, LANES), 0)
    after = lax.broadcasted_iota(jnp.int32, (LANES, LANES), 1)
    upper = jnp.where(before < after, 1.0, 0.0).astype(jnp.bfloat16)
    ones = jnp.ones((LANES, LANES), jnp.bfloat16)
    mask16 = mask.astype(jnp.bfloat16)
    rank = jnp.dot(mask16, upper, preferred_element_type=jnp.float32).astype(jnp.int32)
    count = jnp.dot(mask16, ones, preferred_element_type=jnp.float32).astype(jnp.int32)
    spot = lax.broadcasted_iota(jnp.int32, mask.shape, 1)
    entry = jnp.where(mask > 0.5, (spot - rank) * LANES + spot, spot)
    for bit in range(7):
        width = 1 << bit
        flag = LANES << bit
        moved = pltpu.roll(entry, LANES - width, 1)
        stay = jnp.where((entry & flag) != 0, entry & (LANES - 1), entry)
        entry = jnp.where((moved & flag) != 0, moved, stay)
    entry = entry & (LANES - 1)
    bases = []
    running = jnp.zeros((cells, LANES), jnp.int32)
    table = base_ref[...]
    spot_cells = lax.broadcasted_iota(jnp.int32, (cells, LANES), 1)
    for n in range(len(NEAR)):
        bases.append(running)
        table = jnp.where(spot_cells == n, running, table)
        running = running + count[n * cells : (n + 1) * cells, :]
    base_ref[...] = jnp.where(spot_cells == len(NEAR), running, table)
    base_all = jnp.concatenate(bases, axis=0)
    for bit in range(7):
        width = 1 << bit
        entry = jnp.where((base_all & width) != 0, pltpu.roll(entry, width, 1), entry)
    index_ref[...] = entry


def force_kernel(step_tag, phase, padded_ref, state_ref, *refs):
    if phase == 0:
        tile_out, index_ref, base_ref, *scratch = refs
    elif phase == 1:
        index_ref, base_ref, tile_out, state_out, *scratch = refs
    else:
        index_ref, base_ref, state_out, pos_out, vel_out, *scratch = refs
    rows_x, masks, shifts, base_smem, list_ref, own_wide, force_wide, copy_sem = scratch
    px, py, pz = padded_ref.shape[:3]
    cx, cy, cz = px - 2, py - 2, pz - 2
    cells = cx * cy * cz
    if phase == 0:
        select_beads(padded_ref, rows_x, masks, index_ref, base_ref)
    to_smem = pltpu.make_async_copy(base_ref, base_smem, copy_sem)
    to_smem.start()
    lane = lax.broadcasted_iota(jnp.int32, (ROWS, LANES), 1)
    row_id = lax.broadcasted_iota(jnp.int32, (ROWS, LANES), 0)
    for n, offset in enumerate(NEAR):
        shift = jnp.zeros((ROWS, LANES), jnp.float32)
        for k in range(3):
            shift = jnp.where(row_id == k, cell_edge * offset[k], shift)
        shifts[n] = shift
    force_wide[...] = jnp.zeros(force_wide.shape, jnp.float32)
    zero = jnp.zeros((BLOCK, LANES), jnp.float32)
    to_smem.wait()

    def place(cell):
        return cell // (cy * cz), cell % cy, (cell // cy) % cz

    def prepare(cell, slot):
        ix, iy, iz = place(cell)
        current = jnp.zeros((ROWS, LANES), jnp.float32)
        for n, offset in enumerate(NEAR):
            tile = padded_ref[ix + 1 + offset[0], iy + 1 + offset[1], iz + 1 + offset[2]]
            index = jnp.broadcast_to(index_ref[pl.ds(n * cells + cell, 1), :], (ROWS, LANES))
            found = jnp.take_along_axis(tile, index, axis=1) + shifts[n]
            base = base_smem[cell, n]
            following = base_smem[cell, n + 1]
            merged = jnp.where(lane >= (base & (LANES - 1)), found, current)
            list_ref[slot, base >> 7] = merged
            crossed = (following >> 7) > (base >> 7)
            current = jnp.where(crossed, found, merged)
        total = base_smem[cell, len(NEAR)]
        list_ref[slot, total >> 7] = jnp.where(
            (row_id == 0) & (lane >= (total & (LANES - 1))), -FAR, current
        )
        own_cols = padded_ref[ix + 1, iy + 1, iz + 1].T
        for k in range(7):
            own_wide[slot, k] = jnp.broadcast_to(own_cols[:, k : k + 1], (LANES, LANES))

    prepare(0, 0)

    def one_cell(cell, carry, more=True):
        ix, iy, iz = place(cell)
        slot = cell & 1
        chunks = (base_smem[cell, len(NEAR)] + LANES - 1) >> 7
        blocks = (base_smem[cell, len(NEAR) + 1] + BLOCK - 1) // BLOCK

        def one_block(block, carry):
            at = pl.multiple_of(block * BLOCK, BLOCK)
            own = [own_wide[slot, k, pl.ds(at, BLOCK), :] for k in range(7)]
            own[6] = own[6] * (1.0 / hash_prime)

            def one_chunk(index, sums):
                chunk = [list_ref[slot, index, k : k + 1, :] for k in range(7)]
                terms = pair_terms(own, chunk, step_tag)
                return tuple(sums[k] + terms[k] for k in range(3))

            sums = lax.fori_loop(0, chunks, one_chunk, (zero, zero, zero))
            for k in range(3):
                force_wide[k, pl.ds(at, BLOCK), :] = sums[k]
            return carry

        lax.fori_loop(0, blocks, one_block, 0)
        if more:
            prepare(cell + 1, 1 - slot)
        own_tile = padded_ref[ix + 1, iy + 1, iz + 1]
        wide = force_wide[...].reshape(3 * LANES, LANES)
        coarse = wide.astype(jnp.bfloat16)
        fine = (wide - coarse.astype(jnp.float32)).astype(jnp.bfloat16)
        summed = lax.dot_general(
            jnp.ones((ROWS, 2 * LANES), jnp.bfloat16),
            jnp.concatenate([coarse, fine], axis=1),
            (((1,), (1,)), ((), ())),
            preferred_element_type=jnp.float32,
        )
        state = state_ref[ix, iy, iz]
        new_vel, force = [], []
        for k in range(3):
            row = summed[0:1, k * LANES : (k + 1) * LANES]
            row = jnp.where(own_tile[7:8, :] > 0.5, row, 0.0)
            force.append(row)
            new_vel.append(
                state[k : k + 1, :] + 0.5 * time_step * (state[3 + k : 4 + k, :] + row)
            )
        if phase == 0:
            for k in range(3):
                tile_out[ix, iy, iz, k : k + 1, :] = own_tile[k : k + 1, :]
                tile_out[ix, iy, iz, 3 + k : 4 + k, :] = friction * new_vel[k]
            tile_out[ix, iy, iz, 6:8, :] = own_tile[6:8, :]
            return carry
        for k in range(3):
            state_out[ix, iy, iz, k : k + 1, :] = new_vel[k]
            state_out[ix, iy, iz, 3 + k : 4 + k, :] = force[k]
        state_out[ix, iy, iz, 6:8, :] = state[6:8, :]
        for k in range(3):
            position = own_tile[k : k + 1, :]
            if phase == 2:
                pos_out[k, ix, iy, pl.ds(iz, 1), :] = position
                vel_out[k, ix, iy, pl.ds(iz, 1), :] = new_vel[k]
                continue
            position = position + time_step * new_vel[k]
            position = position + 0.5 * time_step * time_step * force[k]
            tile_out[ix, iy, iz, k : k + 1, :] = position
            guessed = new_vel[k] + predict_weight * time_step * force[k]
            tile_out[ix, iy, iz, 3 + k : 4 + k, :] = friction * guessed
        if phase == 1:
            tile_out[ix, iy, iz, 6:7, :] = centred(state[6:7, :], step_tag + 1)
            tile_out[ix, iy, iz, 7:8, :] = state[7:8, :]
        return carry

    lax.fori_loop(0, cells - 1, one_cell, 0)
    one_cell(jnp.int32(cells - 1), 0, more=False)


def force_call(step_tag, phase, padded, state, *selection):
    px, py, pz = padded.shape[:3]
    cx, cy, cz = state.shape[:3]
    cells = cx * cy * cz
    near = len(NEAR)
    tall = -(-py // 8) * 8
    brick = jax.ShapeDtypeStruct(state.shape, jnp.float32)
    beads = jax.ShapeDtypeStruct((3, cx, cy, cz, LANES), jnp.float32)
    if phase == 0:
        index = jax.ShapeDtypeStruct((near * cells, LANES), jnp.int32)
        outs = (brick, index, jax.ShapeDtypeStruct((cells, LANES), jnp.int32))
    else:
        outs = (brick, brick) if phase == 1 else (brick, beads, beads)
    return pl.pallas_call(
        functools.partial(force_kernel, step_tag, phase),
        out_shape=outs,
        in_specs=[VMEM_SPEC] * (2 + len(selection)),
        out_specs=(VMEM_SPEC,) * len(outs),
        scratch_shapes=[
            pltpu.VMEM((3, px, pz, tall, LANES), jnp.float32),
            pltpu.VMEM((near * cells, LANES), jnp.float32),
            pltpu.VMEM((near, ROWS, LANES), jnp.float32),
            pltpu.SMEM((cells, LANES), jnp.int32),
            pltpu.VMEM((2, near + 1, ROWS, LANES), jnp.float32),
            pltpu.VMEM((2, 7, LANES, LANES), jnp.float32),
            pltpu.VMEM((3, LANES, LANES), jnp.float32),
            pltpu.SemaphoreType.DMA,
        ],
        compiler_params=pltpu.CompilerParams(vmem_limit_bytes=32 * 1024 * 1024),
        name="pair_forces",
    )(padded, state, *selection)


MESH = pl.DeviceIdType.MESH
AROUND = [offset for offset in NEAR if offset != (0, 0, 0)]


def when(condition, body):
    if condition is None:
        body()
    else:
        pl.when(condition)(body)


def beside(offset, sizes):
    nx, ny, nz = sizes
    target = (
        lax.rem(lax.axis_index("gx") + (offset[0] + nx), nx),
        lax.axis_index("gy") + offset[1],
        lax.axis_index("gz") + offset[2],
    )
    exists = None
    for step, place, size in ((offset[1], target[1], ny), (offset[2], target[2], nz)):
        if step != 0:
            inside = place >= 0 if step < 0 else place < size
            exists = inside if exists is None else exists & inside
    return target, exists


def source_slice(step, count):
    return pl.ds(0, count) if step == 0 else pl.ds(count - 1 if step > 0 else 0, 1)


def halo_slice(step, count):
    return pl.ds(1, count) if step == 0 else pl.ds(0 if step > 0 else count + 1, 1)


def exchange_body(sizes, fill, source_ref, padded_ref, send_sems, recv_sems):
    extent = tuple(size - 2 for size in padded_ref.shape[:3])
    barrier = pltpu.get_barrier_semaphore()
    places = {offset: beside(offset, sizes) for offset in AROUND}
    for offset in AROUND:
        target, exists = places[offset]

        def greet(target=target):
            pl.semaphore_signal(barrier, inc=1, device_id=target, device_id_type=MESH)

        when(exists, greet)
    fill()
    copies = {}
    for number, offset in enumerate(AROUND):
        target, exists = places[offset]
        back = tuple(-step for step in offset)
        area = tuple(halo_slice(back[k], extent[k]) for k in range(3))
        if exists is not None:

            def blank(area=area):
                shape = tuple(part.size for part in area) + padded_ref.shape[3:]
                padded_ref[area] = jnp.zeros(shape, jnp.float32)

            pl.when(jnp.logical_not(exists))(blank)
        copies[offset] = pltpu.make_async_remote_copy(
            src_ref=source_ref.at[tuple(source_slice(offset[k], extent[k]) for k in range(3))],
            dst_ref=padded_ref.at[tuple(halo_slice(offset[k], extent[k]) for k in range(3))],
            send_sem=send_sems.at[number],
            recv_sem=recv_sems.at[number],
            device_id=target,
            device_id_type=MESH,
        )
    around = 3
    for axis, size in (("gy", sizes[1]), ("gz", sizes[2])):
        place = lax.axis_index(axis)
        around = around * (1 + jnp.minimum(place, 1) + jnp.minimum(size - 1 - place, 1))
    pl.semaphore_wait(barrier, around - 1)
    for offset in AROUND:
        when(places[offset][1], copies[offset].start)
    for offset in AROUND:
        back = tuple(-step for step in offset)
        when(places[back][1], copies[offset].wait_recv)
    for offset in AROUND:
        when(places[offset][1], copies[offset].wait_send)


def exchange_kernel(sizes, tile_ref, padded_ref, send_sems, recv_sems):
    cx, cy, cz = tile_ref.shape[:3]

    def fill():
        padded_ref[1 : 1 + cx, 1 : 1 + cy, 1 : 1 + cz] = tile_ref[...]

    exchange_body(sizes, fill, tile_ref, padded_ref, send_sems, recv_sems)


def first_kernel(
    sizes, count_hbm, pos_hbm, vel_hbm, force_hbm, seed_hbm, padded_ref, state_ref,
    count_ref, pos_ref, vel_ref, force_ref, seed_ref, load_sems, tile_ref, send_sems, recv_sems,
):
    loads = []
    for number, (source, target) in enumerate(
        (
            (count_hbm, count_ref),
            (pos_hbm, pos_ref),
            (vel_hbm, vel_ref),
            (force_hbm, force_ref),
            (seed_hbm, seed_ref),
        )
    ):
        loads.append(pltpu.make_async_copy(source, target, load_sems.at[number]))
        loads[-1].start()
    cx, cy, cz = tile_ref.shape[:3]
    slot = lax.broadcasted_iota(jnp.int32, (1, LANES), 1)

    def fill():
        for load in loads:
            load.wait()
        for ix in range(cx):
            for iy in range(cy):
                for iz in range(cz):
                    pos, vel, force = [
                        ref[:, ix, iy, iz, :] for ref in (pos_ref, vel_ref, force_ref)
                    ]
                    seed = seed_ref[ix, iy, iz : iz + 1, :].astype(jnp.float32)
                    here = jnp.where(slot < count_ref[ix, iy, iz], 1.0, 0.0)
                    pos = pos + time_step * vel + 0.5 * time_step * time_step * force
                    guessed = vel + predict_weight * time_step * force
                    for ref, top, low, mark in (
                        (tile_ref, pos, friction * guessed, centred(seed, 3)),
                        (state_ref, vel, force, seed),
                    ):
                        ref[ix, iy, iz, 0:3, :] = top
                        ref[ix, iy, iz, 3:6, :] = low
                        ref[ix, iy, iz, 6:7, :] = mark
                        ref[ix, iy, iz, 7:8, :] = here
        padded_ref[1 : 1 + cx, 1 : 1 + cy, 1 : 1 + cz] = tile_ref[...]

    exchange_body(sizes, fill, tile_ref, padded_ref, send_sems, recv_sems)


def mesh_sizes():
    return tuple(lax.axis_size(axis) for axis in ("gx", "gy", "gz"))


def padded_shape(extent):
    return tuple(size + 2 for size in extent) + (ROWS, LANES)


def exchange_sems():
    return [pltpu.SemaphoreType.DMA((len(AROUND),)), pltpu.SemaphoreType.DMA((len(AROUND),))]


def comm_params(number):
    return pltpu.CompilerParams(
        collective_id=number, has_side_effects=True, vmem_limit_bytes=32 * 1024 * 1024
    )


def exchange_call(tile):
    return pl.pallas_call(
        functools.partial(exchange_kernel, mesh_sizes()),
        out_shape=jax.ShapeDtypeStruct(padded_shape(tile.shape[:3]), jnp.float32),
        in_specs=[VMEM_SPEC],
        out_specs=VMEM_SPEC,
        scratch_shapes=exchange_sems(),
        compiler_params=comm_params(1),
        name="exchange",
    )(tile)


def first_call(cell_count, bead_pos, bead_vel, bead_force, pair_seed):
    extent = cell_count.shape
    return pl.pallas_call(
        functools.partial(first_kernel, mesh_sizes()),
        out_shape=(
            jax.ShapeDtypeStruct(padded_shape(extent), jnp.float32),
            jax.ShapeDtypeStruct(extent + (ROWS, LANES), jnp.float32),
        ),
        in_specs=[HBM_SPEC] * 5,
        out_specs=(VMEM_SPEC, VMEM_SPEC),
        scratch_shapes=[
            pltpu.SMEM(extent, jnp.int32),
            pltpu.VMEM(bead_pos.shape, jnp.float32),
            pltpu.VMEM(bead_pos.shape, jnp.float32),
            pltpu.VMEM(bead_pos.shape, jnp.float32),
            pltpu.VMEM(pair_seed.shape, jnp.int32),
            pltpu.SemaphoreType.DMA((5,)),
            pltpu.VMEM(extent + (ROWS, LANES), jnp.float32),
        ]
        + exchange_sems(),
        compiler_params=comm_params(2),
        name="first_exchange",
    )(cell_count, bead_pos, bead_vel, bead_force, pair_seed)


def gather_kernel(
    sizes, state_ref, half_hbm, grid_hbm, map_hbm, whole,
    half_ref, grid_ref, map_ref, load_sems, mine, plane, slots, send_sems, recv_sems,
):
    loads = []
    for number, (source, target) in enumerate(
        ((half_hbm, half_ref), (grid_hbm, grid_ref), (map_hbm, map_ref))
    ):
        loads.append(pltpu.make_async_copy(source, target, load_sems.at[number]))
        loads[-1].start()
    nx, ny, nz = sizes
    cx, cy, cz = state_ref.shape[:3]
    rows, depth = grid_ref.shape[2:]
    span = mine.shape[2]
    count_y = span // depth
    here = (lax.axis_index("gx"), lax.axis_index("gy"), lax.axis_index("gz"))
    barrier = pltpu.get_barrier_semaphore()
    across, along = [], []
    for step_y in range(ny):
        for step_z in range(nz):
            if step_y + step_z > 0:
                place_y = lax.rem(here[1] + step_y, ny)
                across.append((here[0], place_y, lax.rem(here[2] + step_z, nz)))
    for step in range(1, nx):
        along.append((lax.rem(here[0] + step, nx), here[1], here[2]))
    for target in across + along:
        pl.semaphore_signal(barrier, inc=1, device_id=target, device_id_type=MESH)

    for load in loads:
        load.wait()
    lane = lax.broadcasted_iota(jnp.int32, (ROWS, span), 1)
    row_id = lax.broadcasted_iota(jnp.int32, (ROWS, LANES), 0)
    for ix in range(cx):
        placed = jnp.zeros((ROWS, span), jnp.float32)
        for row in range(rows):
            mine[ix] = jnp.zeros((ROWS, span), jnp.float32)
            for k in range(3):
                mine[ix, 4 + k : 5 + k, 0:depth] = grid_ref[k, ix, row : row + 1, :]
            mine[ix, 7:8, 0:depth] = map_ref[ix, row : row + 1, :].astype(jnp.float32)
            at = ((here[1] * nz + here[2]) * rows + row) * depth
            placed = placed + pltpu.roll(mine[ix], at, 1)
        for iy in range(cy):
            for iz in range(cz):
                tile = state_ref[ix, iy, iz]
                values = jnp.where(row_id < 3, tile, jnp.where(row_id == 3, 1.0, 0.0))
                values = jnp.where(tile[7:8, :] > 0.5, values, 0.0)
                half = half_ref[ix, iy, iz : iz + 1, :]
                for side in (0, 1):
                    total = jnp.sum(
                        jnp.where(half == side, values, 0.0), axis=1, keepdims=True
                    )
                    at = (here[1] * cy + iy) * depth + (here[2] * cz + iz) * 2 + side
                    placed = placed + jnp.where(lane == at, total, 0.0)
        mine[ix] = placed

    pl.semaphore_wait(barrier, len(across) + len(along))

    def send_all(targets, source, landings, first):
        copies = []
        for number, target in enumerate(targets):
            copies.append(
                pltpu.make_async_remote_copy(
                    src_ref=source,
                    dst_ref=landings[number],
                    send_sem=send_sems.at[first + number],
                    recv_sem=recv_sems.at[first + number],
                    device_id=target,
                    device_id_type=MESH,
                )
            )
        for copy in copies:
            copy.start()
        return copies

    copies = send_all(across, mine, [slots.at[k] for k in range(len(across))], 0)
    for copy in copies:
        copy.wait_recv()
    total = mine[...]
    for number in range(len(across)):
        total = total + slots[number]
    plane[...] = total
    band = pl.ds(here[0] * cx, cx)
    later = send_all(along, plane, [whole.at[band]] * len(along), len(across))
    whole[band] = total
    for copy in later:
        copy.wait()
    for copy in copies:
        copy.wait_send()


def project_kernel(sizes, extent, rows, depth, whole, grid_out, pressure_out, brick_out, fields):
    nx, ny, nz = sizes
    cx, cy, cz = extent
    span = whole.shape[2]
    count_y = span // depth
    here = (lax.axis_index("gx"), lax.axis_index("gy"), lax.axis_index("gz"))
    parts = [whole[:, k, :] for k in range(8)]
    lanes = lax.broadcasted_iota(jnp.int32, parts[0].shape, 1)
    place_z = lax.rem(lanes, depth)
    place_y = lanes // depth
    count_x = parts[0].shape[0]

    def after(field, axis):
        if axis == 0:
            return pltpu.roll(field, count_x - 1, 0)
        if axis == 1:
            return jnp.where(place_y == count_y - 1, 0.0, pltpu.roll(field, span - depth, 1))
        return jnp.where(place_z == depth - 1, 0.0, pltpu.roll(field, span - 1, 1))

    def prior(field, axis):
        if axis == 0:
            return pltpu.roll(field, 1, 0)
        if axis == 1:
            return jnp.where(place_y == 0, 0.0, pltpu.roll(field, depth, 1))
        return jnp.where(place_z == 0, 0.0, pltpu.roll(field, 1, 1))

    def total_of(field):
        return jnp.sum(jnp.sum(field, axis=0, keepdims=True), axis=1, keepdims=True)

    share = jnp.maximum(parts[3], 1.0)
    coupled = [
        parts[4 + k] + couple_rate * parts[7] * (parts[k] / share - parts[4 + k])
        for k in range(3)
    ]
    divergence = 0.0
    for k in range(3):
        divergence = divergence + after(coupled[k], k) - prior(coupled[k], k)
    residual = -0.5 * divergence
    direction = residual
    pressure = jnp.zeros_like(residual)
    norm_now = total_of(residual * residual)
    for repeat in range(ITERS):
        around = 0.0
        for k in range(3):
            around = around + after(direction, k) + prior(direction, k)
        applied = 6.0 * direction - around
        step_length = norm_now / total_of(direction * applied)
        pressure = pressure + step_length * direction
        residual = residual - step_length * applied
        norm_next = total_of(residual * residual)
        direction = residual + norm_next / norm_now * direction
        norm_now = norm_next
    for k in range(3):
        fields[:, k, :] = coupled[k] - 0.5 * (after(pressure, k) - prior(pressure, k))
    fields[:, 3, :] = pressure
    for ix in range(cx):
        own = fields[here[0] * cx + ix]
        for row in range(rows):
            start = ((here[1] * nz + here[2]) * rows + row) * depth
            band = pltpu.roll(own, lax.rem(span - start, span), 1)
            for k in range(3):
                grid_out[k, ix, row : row + 1, :] = band[k : k + 1, 0:depth]
            pressure_out[ix, row : row + 1, :] = band[3:4, 0:depth]
        for iy in range(cy):
            start = (here[1] * cy + iy) * depth + here[2] * cz * 2
            band = pltpu.roll(own, lax.rem(span - start, span), 1)
            for k in range(3):
                brick_out[k, ix, iy : iy + 1, :] = band[k : k + 1, 0 : cz * 2]


def project_call(state, bead_half, grid_vel, correlation_map):
    sizes = mesh_sizes()
    nx, ny, nz = sizes
    cx, cy, cz = state.shape[:3]
    depth = grid_vel.shape[3]
    span = ny * cy * depth
    shape = (cx, ROWS, span)
    across = max(ny * nz - 1, 1)
    peers = max(ny * nz + nx - 2, 1)
    whole = jax.ShapeDtypeStruct((nx * cx, ROWS, span), jnp.float32)
    gathered = pl.pallas_call(
        functools.partial(gather_kernel, sizes),
        out_shape=whole,
        in_specs=[VMEM_SPEC] + [HBM_SPEC] * 3,
        out_specs=VMEM_SPEC,
        scratch_shapes=[
            pltpu.VMEM(bead_half.shape, jnp.int32),
            pltpu.VMEM(grid_vel.shape, jnp.float32),
            pltpu.VMEM(correlation_map.shape, jnp.int32),
            pltpu.SemaphoreType.DMA((3,)),
            pltpu.VMEM(shape, jnp.float32),
            pltpu.VMEM(shape, jnp.float32),
            pltpu.VMEM((across,) + shape, jnp.float32),
            pltpu.SemaphoreType.DMA((peers,)),
            pltpu.SemaphoreType.DMA((peers,)),
        ],
        compiler_params=comm_params(3),
        name="gather_grid",
    )(state, bead_half, grid_vel, correlation_map)
    return pl.pallas_call(
        functools.partial(project_kernel, sizes, (cx, cy, cz), grid_vel.shape[2], depth),
        out_shape=(
            jax.ShapeDtypeStruct(grid_vel.shape, jnp.float32),
            jax.ShapeDtypeStruct(correlation_map.shape, jnp.float32),
            jax.ShapeDtypeStruct((3, cx, cy, cz * 2), jnp.float32),
        ),
        in_specs=[VMEM_SPEC],
        out_specs=(VMEM_SPEC,) * 3,
        scratch_shapes=[pltpu.VMEM(whole.shape, jnp.float32)],
        compiler_params=pltpu.CompilerParams(vmem_limit_bytes=32 * 1024 * 1024),
        name="project",
    )(gathered)


def per_device(
    bead_pos, bead_vel, bead_force, cell_count, pair_seed, bead_half, grid_vel, correlation_map
):
    padded, state = first_call(cell_count, bead_pos, bead_vel, bead_force, pair_seed)
    for step_number in range(STEPS):
        step_tag = step_number + 3
        if step_number > 0:
            padded = exchange_call(tile)
        tile, *selection = force_call(step_tag, 0, padded, state)
        padded = exchange_call(tile)
        if step_number < STEPS - 1:
            tile, state = force_call(step_tag, 1, padded, state, *selection)
    state, position, velocity = force_call(step_tag, 2, padded, state, *selection)
    return (position, velocity, *project_call(state, bead_half, grid_vel, correlation_map))


def solution(mesh):
    placed = (
        P(None, "gx", "gy", "gz", None),
        P(None, "gx", "gy", "gz", None),
        P(None, "gx", "gy", "gz", None),
        P("gx", "gy", "gz"),
        P("gx", "gy", "gz", None),
        P("gx", "gy", "gz", None),
        P(None, "gx", ("gy", "gz"), None),
        P("gx", ("gy", "gz"), None),
    )
    return jax.shard_map(
        per_device,
        mesh=mesh,
        in_specs=placed,
        out_specs=(
            P(None, "gx", "gy", "gz", None),
            P(None, "gx", "gy", "gz", None),
            P(None, "gx", ("gy", "gz"), None),
            P("gx", ("gy", "gz"), None),
            P(None, "gx", "gy", "gz"),
        ),
        check_vma=False,
    )
```
